256 devices in a mesh: texel: 16 (over x, y), light: 4 (over z_hi), view: 4 (over z_lo, core).
Axes of the slice: x: 4, y: 4, z: 8 (z_hi: 4, z_lo: 2; z = z_hi * 2 + z_lo), core: 2. Of those that a mesh axis runs over, the one named last changes fastest.
Arguments:
- slab: bfloat16 [80, 80, 16384], P('light', 'view', 'texel'), may hold values from -6 to 6
- basis: bfloat16 [80, 48], P('view'), may hold values from -0.625 to 0.625
Outputs:
- view_gram: float32 [80, 80], P('view')
- core: bfloat16 [48, 80, 16384], P('view', 'light', 'texel')
- light_gram: float32 [80, 80], P('light')
The draws below stay inside these ranges and needn't reach their ends.
All inputs are finite; a program needn't handle non-finite values.
Results may differ from the reference program's by a relative error of at most 0.001.
Values may be sent and summed in bfloat16 or wider, within the bound.
A program may use at most 64 MiB of HBM per device.

```python
import jax
import jax.numpy as jnp
from jax import lax

LIGHTS = 80
VIEWS = 80
RANK = 48
COLUMNS = 16384


def block_levels(stream_key, shape, pieces, smallest, top_value):
    level, own = 1.0, jax.random.fold_in(stream_key, 6)
    for position, shards_of in pieces:
        heights = jnp.exp(jax.random.uniform(jax.random.fold_in(own, position), (shards_of,), jnp.float32, smallest / len(pieces), top_value / len(pieces)))
        level = level * jnp.repeat(heights, shape[position] // shards_of).reshape([-1 if axis == position else 1 for axis in range(len(shape))])
    return level


def noise(key, extent, width, bound, split=(), kind=jnp.bfloat16):
    entries = width * jax.random.normal(key, extent, jnp.float32)
    if split:
        entries = entries * block_levels(key, extent, split, -0.22, 0.18)
    return jnp.clip(entries, -bound, bound).astype(kind)


def setup_inputs(seed: int = 0) -> dict:
    key_of = jax.random.split(jax.random.key(seed), 3)
    slab = noise(key_of[0], (LIGHTS, VIEWS, COLUMNS), 1.0, 6.0, ((0, 4), (1, 4), (2, 16)))
    basis = noise(key_of[1], (VIEWS, RANK), VIEWS ** -0.5, 0.625, ((0, 4),))
    return dict(slab=slab, basis=basis)


def reference(slab, basis):
    def view_part(total, page):
        return total + jnp.dot(page, page.T, preferred_element_type=jnp.float32), None

    view_gram, unused = lax.scan(view_part, jnp.zeros((VIEWS, VIEWS), jnp.float32), slab)
    view_gram = view_gram / (LIGHTS * COLUMNS)
    basis_turned = basis.T

    def truncate(page):
        return jnp.dot(basis_turned, page, preferred_element_type=jnp.float32).astype(jnp.bfloat16)

    core_lights = lax.map(truncate, slab)
    flat = core_lights.reshape(LIGHTS, RANK * COLUMNS)
    light_gram = lax.dot_general(flat, flat, (((1,), (1,)), ((), ())), preferred_element_type=jnp.float32)
    light_gram = light_gram / (RANK * COLUMNS)
    return view_gram, jnp.transpose(core_lights, (1, 0, 2)), light_gram
```

```python
import functools

import jax
import jax.numpy as jnp
import numpy as np
from jax import lax
from jax.experimental import pallas as pl
from jax.experimental.pallas import tpu as pltpu
from jax.sharding import PartitionSpec as P

MESH = pl.DeviceIdType.MESH
BF = jnp.bfloat16
F32 = jnp.float32
LB = 20
VB = 20
NV = 4
NL = 4
RB = 12
CB = 256
ROWS = LB * VB
PIECE = RB * LB
GROUP = 80
PAGES = NL * NV


def constants():
    expand = np.zeros((NV * 32, NV * ROWS), np.float32)
    for s in range(NV):
        for l in range(LB):
            for v in range(VB):
                expand[s * 32 + v, s * ROWS + l * VB + v] = 1
    spread = np.zeros((NV * PIECE, 128), np.float32)
    for r in range(NV * RB):
        spread[r * LB : (r + 1) * LB, r] = 1
    rows = np.arange(GROUP)[:, None] % LB
    columns = (np.arange(NV * ROWS)[None, :] // VB) % LB
    mask = (rows == columns).astype(np.float32)
    index = np.arange(4 * GROUP)
    repeat = (index // 20) % 4
    keep = (repeat[:, None] == repeat[None, :]).astype(np.float32)
    item = (index // GROUP) * 20 + index % 20
    pick = np.zeros((2, 8 * PAGES, 4 * GROUP), np.float32)
    for p in range(PAGES):
        for q in range(5):
            pick[0, 8 * p + q] = item == 5 * (NL * (p % NV) + p // NV) + q
            pick[1, 8 * p + q] = item == 5 * p + q
    gather = (item[:, None] == np.arange(128)[None, :]).astype(np.float32)
    return expand, spread, mask, keep, pick, gather


def odd_share(k, t):
    return lax.rem(lax.div(k + 1 - t, 2), 2)


def share_of(k, j):
    e, t = lax.div(j, 2), lax.rem(j, 2)
    return 2 * t + lax.rem(odd_share(k, t) + 1 - e, 2)


def member_for(k, b):
    t, u = lax.div(b, 2), lax.rem(b, 2)
    return 2 * lax.rem(odd_share(k, t) + 1 + u, 2) + t


def center_of(b, n):
    t, u = lax.div(b, 2), lax.rem(b, 2)
    z = lax.rem(1 + 4 * u + 2 * t + lax.div(n, 2), 8)
    return lax.div(z, 2), 2 * lax.rem(z, 2) + lax.rem(n, 2)


def split_dot(a, b):
    def parts(x):
        hi = x.astype(BF)
        rest = x - hi.astype(F32)
        mid = rest.astype(BF)
        return hi, mid, (rest - mid.astype(F32)).astype(BF)

    if a.dtype == BF:
        return sum(jnp.dot(a, p, preferred_element_type=F32) for p in parts(b))
    return sum(jnp.dot(p, b, preferred_element_type=F32) for p in parts(a))


def kernel(
    view_scale, light_scale,
    slab_ref, basis_ref, expand_ref, spread_ref, mask_ref, keep_ref, pick_ref, gather_ref,
    view_ref, core_ref, light_ref,
    dense, share, own_basis, all_basis, weights, pieces, core_land, light_land,
    pages, pages_land, part, part_land, last, last_view, last_light,
    basis_send, basis_recv, slab_send, slab_recv, core_send, core_recv,
    light_send, light_recv, z_send, z_recv, t_send, t_recv, v_send, v_recv, l_send, l_recv,
):
    texels = lax.axis_size("texel")
    tex, i, j = lax.axis_index("texel"), lax.axis_index("light"), lax.axis_index("view")
    me = i * NV + j
    mine = share_of(i, j)

    barrier = pltpu.get_barrier_semaphore()

    def greet_z(o, c):
        other = lax.rem(me + o, PAGES)
        pl.semaphore_signal(
            barrier, inc=1, device_id=(tex, lax.div(other, NV), lax.rem(other, NV)), device_id_type=MESH
        )
        return c

    def greet_t(o, c):
        pl.semaphore_signal(barrier, inc=1, device_id=(lax.rem(tex + o, texels), i, j), device_id_type=MESH)
        return c

    lax.fori_loop(1, PAGES, greet_z, 0)
    lax.fori_loop(1, texels, greet_t, 0)

    own_basis[...] = jnp.zeros_like(own_basis)
    own_basis[0:VB, 0 : NV * RB] = basis_ref[...]
    for l in range(LB):
        dense[l * VB : (l + 1) * VB, :] = slab_ref[l]

    pl.semaphore_wait(barrier, PAGES - 1 + texels - 1)

    def remote(src, dst, send, recv, device):
        return pltpu.make_async_remote_copy(
            src_ref=src, dst_ref=dst, send_sem=send, recv_sem=recv, device_id=device, device_id_type=MESH
        )

    sends = []
    for o in (2, 3, 1):
        other = lax.rem(j + o, NV)
        sends.append(remote(own_basis, all_basis.at[j], basis_send.at[o], basis_recv.at[j], (tex, i, other)))
        sends[-1].start()
    for o in (2, 3, 1):
        other = lax.rem(j + o, NV)
        columns = pl.ds(pl.multiple_of(share_of(i, other) * CB, CB), CB)
        sends.append(
            remote(
                dense.at[:, columns], share.at[pl.ds(pl.multiple_of(j * ROWS, 16), ROWS), :],
                slab_send.at[o], slab_recv.at[j], (tex, i, other),
            )
        )
        sends[-1].start()
    columns = pl.ds(pl.multiple_of(mine * CB, CB), CB)
    local = pltpu.make_async_copy(
        dense.at[:, columns], share.at[pl.ds(pl.multiple_of(j * ROWS, 16), ROWS), :], slab_recv.at[j]
    )
    local.start()
    all_basis[j] = own_basis[...]
    for o in (1, 2, 3):
        other = lax.rem(j + o, NV)
        remote(
            own_basis, all_basis.at[other], basis_send.at[o], basis_recv.at[other], (tex, i, other)
        ).wait_recv()

    stacked = all_basis[...].reshape(NV * 32, 128)
    table = lax.dot_general(
        stacked, expand_ref[...], (((0,), (0,)), ((), ())), preferred_element_type=F32
    ).astype(BF)

    def weight_rows(g, c):
        at = pl.ds(pl.multiple_of(g * GROUP, 16), GROUP)
        full = jnp.dot(spread_ref[at, :], table, preferred_element_type=F32)
        weights[at, :] = full.astype(BF) * mask_ref[...]
        return c

    lax.fori_loop(0, NV * PIECE // GROUP, weight_rows, 0)

    local.wait()
    for o in (1, 2, 3):
        other = lax.rem(j + o, NV)
        at = pl.ds(pl.multiple_of(other * ROWS, 16), ROWS)
        remote(
            dense.at[:, columns], share.at[at, :], slab_send.at[o], slab_recv.at[other], (tex, i, other)
        ).wait_recv()

    for o in (2, 3, 1, 0):
        p = lax.rem(j + o, NV)
        at = pl.ds(pl.multiple_of(p * PIECE, 16), PIECE)
        pieces[at, :] = jnp.dot(weights[at, :], share[...], preferred_element_type=F32).astype(BF)
        ci, cj = center_of(mine, p)
        here = jnp.logical_and(ci == i, cj == j)

        @pl.when(here)
        def _():
            pltpu.make_async_copy(pieces.at[at, :], light_land.at[i], light_recv.at[i]).start()

        @pl.when(jnp.logical_not(here))
        def _():
            remote(pieces.at[at, :], light_land.at[i], light_send.at[o], light_recv.at[i], (tex, ci, cj)).start()

        if o:
            copy = remote(
                pieces.at[at, :], core_land.at[:, columns], core_send.at[o], core_recv.at[j], (tex, i, p)
            )
            sends.append(copy)
        else:
            copy = pltpu.make_async_copy(pieces.at[at, :], core_land.at[:, columns], core_recv.at[j])
        copy.start()

    def gram(blocks, which):
        total = None
        for block in blocks:
            term = lax.dot_general(block, block, (((1,), (1,)), ((), ())), preferred_element_type=F32)
            total = term if total is None else total + term
        rows = split_dot(pick_ref[which], total * keep_ref[...])
        return split_dot(rows, gather_ref[...])

    view_part = gram(
        (jnp.concatenate([share[s * ROWS + g * GROUP : s * ROWS + (g + 1) * GROUP, :] for s in range(NV)], axis=0)
        for g in range(ROWS // GROUP)), 0
    )
    pages[:, 0:8, :] = view_part.reshape(PAGES, 8, 128)

    for k in range(NL):
        pltpu.make_async_copy(pieces.at[pl.ds(0, PIECE), :], light_land.at[k], light_recv.at[k]).wait()
    light_part = gram(
        (jnp.concatenate([light_land[k, g * GROUP : (g + 1) * GROUP, :] for k in range(NL)], axis=0)
        for g in range(PIECE // GROUP)), 1
    )
    pages[:, 8:16, :] = light_part.reshape(PAGES, 8, 128)

    def z_copy(o, slot):
        other = lax.rem(me + o, PAGES)
        return remote(
            pages.at[other], pages_land.at[slot(other)], z_send.at[o], z_recv.at[slot(other)],
            (tex, lax.div(other, NV), lax.rem(other, NV)),
        )

    def z_start(o, c):
        z_copy(o, lambda other: me).start()
        return c

    def z_wait(o, c):
        z_copy(o, lambda other: other).wait_recv()
        return c

    lax.fori_loop(1, PAGES, z_start, 0)
    pages_land[me] = pages[me]
    lax.fori_loop(1, PAGES, z_wait, 0)
    part[...] = jnp.sum(pages_land[...], axis=0)

    def t_copy(o, slot):
        other = lax.rem(tex + o, texels)
        return remote(part, part_land.at[slot(other)], t_send.at[o], t_recv.at[slot(other)], (other, i, j))

    def t_start(o, c):
        t_copy(o, lambda other: tex).start()
        return c

    def t_wait(o, c):
        t_copy(o, lambda other: other).wait_recv()
        return c

    lax.fori_loop(1, texels, t_start, 0)
    part_land[tex] = part[...]
    lax.fori_loop(1, texels, t_wait, 0)
    last[...] = jnp.sum(part_land[...], axis=0)

    def v_copy(o, slot):
        other = lax.rem(i + o, NL)
        return remote(last.at[0:8], last_view.at[slot(other)], v_send.at[o], v_recv.at[slot(other)], (tex, other, j))

    def l_copy(o, slot):
        other = lax.rem(j + o, NV)
        return remote(
            last.at[8:16], last_light.at[slot(other)], l_send.at[o], l_recv.at[slot(other)], (tex, i, other)
        )

    for o in (1, 2, 3):
        v_copy(o, lambda other: i).start()
        l_copy(o, lambda other: j).start()
    last_view[i] = last[0:8]
    last_light[j] = last[8:16]

    pltpu.make_async_copy(pieces.at[pl.ds(0, PIECE), :], core_land.at[:, columns], core_recv.at[j]).wait()
    for o in (1, 2, 3):
        other = lax.rem(j + o, NV)
        theirs = pl.ds(pl.multiple_of(share_of(i, other) * CB, CB), CB)
        remote(
            pieces.at[pl.ds(0, PIECE), :], core_land.at[:, theirs], core_send.at[o], core_recv.at[other],
            (tex, i, other),
        ).wait_recv()
    core_ref[...] = core_land[...]

    for o in (1, 2, 3):
        v_copy(o, lambda other: other).wait_recv()
        l_copy(o, lambda other: other).wait_recv()
    for q in range(4):
        view_ref[5 * q : 5 * q + 5, :] = last_view[q, 0:5, 0:80] * view_scale
        light_ref[5 * q : 5 * q + 5, :] = last_light[q, 0:5, 0:80] * light_scale

    for copy in sends:
        copy.wait_send()
    for o in range(NV):
        p = lax.rem(j + o, NV)
        ci, cj = center_of(mine, p)
        at = pl.ds(pl.multiple_of(p * PIECE, 16), PIECE)

        @pl.when(jnp.logical_not(jnp.logical_and(ci == i, cj == j)))
        def _():
            remote(
                pieces.at[at, :], light_land.at[i], light_send.at[o], light_recv.at[i], (tex, ci, cj)
            ).wait_send()

    def send_waits(o, c):
        z_copy(o, lambda other: me).wait_send()
        t_copy(o, lambda other: tex).wait_send()
        return c

    lax.fori_loop(1, PAGES, send_waits, 0)
    for o in (1, 2, 3):
        v_copy(o, lambda other: i).wait_send()
        l_copy(o, lambda other: j).wait_send()


def body(slab, basis):
    texels = lax.axis_size("texel")
    columns_all = slab.shape[2] * texels
    view_scale = 1.0 / (LB * NL * columns_all)
    light_scale = 1.0 / (RB * NV * columns_all)
    tables = constants()
    tables = [jnp.asarray(x, F32 if n == 3 else BF) for n, x in enumerate(tables)]
    vmem = pl.BlockSpec(memory_space=pltpu.VMEM)
    dma = pltpu.SemaphoreType.DMA
    view_gram, core, light_gram = pl.pallas_call(
        functools.partial(kernel, view_scale, light_scale),
        out_shape=(
            jax.ShapeDtypeStruct((VB, 80), F32),
            jax.ShapeDtypeStruct((PIECE, 4 * CB), BF),
            jax.ShapeDtypeStruct((LB, 80), F32),
        ),
        in_specs=[vmem] * 8,
        out_specs=(vmem,) * 3,
        scratch_shapes=[
            pltpu.VMEM((ROWS, 4 * CB), BF),
            pltpu.VMEM((NV * ROWS, CB), BF),
            pltpu.VMEM((32, 128), BF),
            pltpu.VMEM((NV, 32, 128), BF),
            pltpu.VMEM((NV * PIECE, NV * ROWS), BF),
            pltpu.VMEM((NV * PIECE, CB), BF),
            pltpu.VMEM((PIECE, 4 * CB), BF),
            pltpu.VMEM((NL, PIECE, CB), BF),
            pltpu.VMEM((PAGES, 16, 128), F32),
            pltpu.VMEM((PAGES, 16, 128), F32),
            pltpu.VMEM((16, 128), F32),
            pltpu.VMEM((texels, 16, 128), F32),
            pltpu.VMEM((16, 128), F32),
            pltpu.VMEM((NL, 8, 128), F32),
            pltpu.VMEM((NV, 8, 128), F32),
            dma((NV,)), dma((NV,)), dma((NV,)), dma((NV,)), dma((NV,)), dma((NV,)),
            dma((NV,)), dma((NL,)), dma((PAGES,)), dma((PAGES,)), dma((texels,)), dma((texels,)),
            dma((NL,)), dma((NL,)), dma((NV,)), dma((NV,)),
        ],
        compiler_params=pltpu.CompilerParams(
            collective_id=0, has_side_effects=True, vmem_limit_bytes=48 * 1024 * 1024
        ),
    )(slab, basis, *tables)
    return view_gram, core.reshape(RB, LB, 4 * CB), light_gram


def solution(mesh):
    return jax.shard_map(
        body,
        mesh=mesh,
        in_specs=(P("light", "view", "texel"), P("view", None)),
        out_specs=(P("view", None), P("view", "light", "texel"), P("light", None)),
        check_vma=False,
    )
```

```python
import functools

import jax
import jax.numpy as jnp
from jax import lax
from jax.experimental import pallas as pl
from jax.experimental.pallas import tpu as pltpu
from jax.sharding import PartitionSpec as P

MESH = pl.DeviceIdType.MESH
BF = jnp.bfloat16
F32 = jnp.float32
LB = 20
VB = 20
NV = 4
NL = 4
RB = 12
CB = 256
HB = CB // 2
ROWS = LB * VB
PIECE = RB * LB
GROUP = 80
PAGES = NL * NV


def cells(shape):
    return lax.broadcasted_iota(jnp.int32, shape, 0), lax.broadcasted_iota(jnp.int32, shape, 1)


def div20(x):
    return (x * 3277) >> 16


def ones_where(condition, dtype=BF):
    return jnp.where(condition, 1.0, 0.0).astype(dtype)


def expand_table():
    row, col = cells((NV * 32, NV * ROWS))
    line = div20(col)
    return ones_where(row == 32 * div20(line) + col - VB * line)


def light_mask():
    row, col = cells((GROUP, NV * ROWS))
    line = div20(col)
    return ones_where(row - LB * div20(row) == line - LB * div20(line))


def spread_rows(g):
    row, col = cells((GROUP, 128))
    return ones_where(div20(row) + 4 * g == col)


def item(x):
    line = div20(x)
    return 20 * (line >> 2) + x - 20 * line


def keep_table():
    row, col = cells((4 * GROUP, 4 * GROUP))
    return (div20(row) & 3) == (div20(col) & 3)


def pick_table(turned):
    row, col = cells((8 * PAGES, 4 * GROUP))
    p, q = row >> 3, row & 7
    if turned:
        p = NL * (p & 3) + (p >> 2)
    return ones_where((q < 5) & (5 * p + q == item(col)))


def gather_table():
    row, col = cells((4 * GROUP, 128))
    return ones_where(item(row) == col)


def odd_share(k, t):
    return lax.rem(lax.div(k + 1 - t, 2), 2)


def share_of(k, j):
    e, t = lax.div(j, 2), lax.rem(j, 2)
    return 2 * t + lax.rem(odd_share(k, t) + 1 - e, 2)


def member_for(k, b):
    t, u = lax.div(b, 2), lax.rem(b, 2)
    return 2 * lax.rem(odd_share(k, t) + 1 + u, 2) + t


def center_of(b, n):
    t, u = lax.div(b, 2), lax.rem(b, 2)
    z = lax.rem(1 + 4 * u + 2 * t + lax.div(n, 2), 8)
    return lax.div(z, 2), 2 * lax.rem(z, 2) + lax.rem(n, 2)


def split_dot(a, b):
    def parts(x):
        hi = x.astype(BF)
        rest = x - hi.astype(F32)
        mid = rest.astype(BF)
        return hi, mid, (rest - mid.astype(F32)).astype(BF)

    if a.dtype == BF:
        return sum(jnp.dot(a, p, preferred_element_type=F32) for p in parts(b))
    return sum(jnp.dot(p, b, preferred_element_type=F32) for p in parts(a))


def remote(src, dst, send, recv, device):
    return pltpu.make_async_remote_copy(
        src_ref=src, dst_ref=dst, send_sem=send, recv_sem=recv, device_id=device, device_id_type=MESH
    )


def kernel(
    view_scale, light_scale,
    slab_hbm, basis_hbm,
    view_ref, core_ref, light_ref,
    slab_ref, basis_ref, mask_ref, dense, share, own_basis, all_basis, weights, pieces, core_land, light_land,
    pages, z_land, part, t_land, whole, last_land,
    load, basis_send, basis_recv, slab_send, slab_recv, core_send, core_recv,
    light_send, light_recv, z_send, z_recv, t_send, t_recv, last_send, last_recv,
):
    texels = lax.axis_size("texel")
    tex, i, j = lax.axis_index("texel"), lax.axis_index("light"), lax.axis_index("view")
    me = i * NV + j
    mine = share_of(i, j)

    load_slab = pltpu.make_async_copy(slab_hbm, slab_ref, load.at[0])
    load_basis = pltpu.make_async_copy(basis_hbm, basis_ref, load.at[1])
    load_slab.start()
    load_basis.start()
    barrier = pltpu.get_barrier_semaphore()

    def greet_z(o, c):
        other = lax.rem(me + o, PAGES)
        pl.semaphore_signal(
            barrier, inc=1, device_id=(tex, lax.div(other, NV), lax.rem(other, NV)), device_id_type=MESH
        )
        return c

    def greet_t(o, c):
        pl.semaphore_signal(barrier, inc=1, device_id=(lax.rem(tex + o, texels), i, j), device_id_type=MESH)
        return c

    lax.fori_loop(1, PAGES, greet_z, 0)
    lax.fori_loop(1, texels, greet_t, 0)

    own_basis[...] = jnp.zeros_like(own_basis)
    load_basis.wait()
    own_basis[0:VB, 0 : NV * RB] = basis_ref[...]
    load_slab.wait()
    for n in range(2 * NV):
        for l in range(LB):
            dense[n, l * VB : (l + 1) * VB, :] = slab_ref[l, :, n * HB : (n + 1) * HB]

    pl.semaphore_wait(barrier, PAGES - 1 + texels - 1)

    others = [lax.rem(j + o, NV) for o in range(NV)]
    shares = [share_of(i, other) for other in others]

    def rows_of(source):
        return pl.ds(pl.multiple_of(source * ROWS, 16), ROWS)

    def piece_of(p):
        return pl.ds(pl.multiple_of(p * PIECE, 16), PIECE)

    def slab_copy(h, o, slot):
        return remote(
            dense.at[2 * shares[o] + h], share.at[h, rows_of(slot), :], slab_send.at[h, o], slab_recv.at[h, slot],
            (tex, i, others[o]),
        )

    def basis_copy(o, slot):
        return remote(own_basis, all_basis.at[slot], basis_send.at[o], basis_recv.at[slot], (tex, i, others[o]))

    for o in (2, 3, 1):
        basis_copy(o, j).start()
    local = []
    for h in range(2):
        for o in (2, 3, 1):
            slab_copy(h, o, j).start()
        local.append(
            pltpu.make_async_copy(dense.at[2 * mine + h], share.at[h, rows_of(j), :], slab_recv.at[h, j])
        )
        local[-1].start()
    all_basis[j] = own_basis[...]
    for o in (1, 2, 3):
        basis_copy(o, others[o]).wait_recv()

    table = lax.dot_general(
        all_basis[...].reshape(NV * 32, 128), expand_table(), (((0,), (0,)), ((), ())), preferred_element_type=F32
    ).astype(BF)
    mask_ref[...] = light_mask()

    def weight_rows(g, c):
        at = pl.ds(pl.multiple_of(g * GROUP, 16), GROUP)
        full = jnp.dot(spread_rows(g), table, preferred_element_type=F32)
        weights[at, :] = full.astype(BF) * mask_ref[...]
        return c

    lax.fori_loop(0, NV * PIECE // GROUP, weight_rows, 0)

    def light_copy(h, o, ci, cj):
        return remote(
            pieces.at[h, piece_of(others[o]), :], light_land.at[h, i], light_send.at[h, o], light_recv.at[h, i],
            (tex, ci, cj),
        )

    def core_copy(h, o, slot, place):
        return remote(
            pieces.at[h, piece_of(others[o]), :], core_land.at[2 * place + h], core_send.at[h, o],
            core_recv.at[h, slot], (tex, i, others[o]),
        )

    centers = [center_of(mine, p) for p in others]
    for h in range(2):
        local[h].wait()
        for o in (1, 2, 3):
            slab_copy(h, o, others[o]).wait_recv()
        for o in (2, 3, 1, 0):
            at = piece_of(others[o])
            pieces[h, at, :] = jnp.dot(weights[at, :], share[h], preferred_element_type=F32).astype(BF)
            ci, cj = centers[o]
            here = jnp.logical_and(ci == i, cj == j)

            @pl.when(here)
            def _():
                pltpu.make_async_copy(pieces.at[h, at, :], light_land.at[h, i], light_recv.at[h, i]).start()

            @pl.when(jnp.logical_not(here))
            def _():
                light_copy(h, o, ci, cj).start()

    def products(stacks):
        total = None
        for stack in stacks:
            term = lax.dot_general(stack, stack, (((1,), (1,)), ((), ())), preferred_element_type=F32)
            total = term if total is None else total + term
        return total

    def to_pages(total, turned):
        rows = split_dot(pick_table(turned), jnp.where(keep_table(), total, 0.0))
        return split_dot(rows, gather_table()).reshape(PAGES, 8, 128)

    def z_copy(g, o, slot):
        other = lax.rem(me + o, PAGES)
        return remote(
            pages.at[g, other], z_land.at[g, slot(other)], z_send.at[g, o], z_recv.at[g, slot(other)],
            (tex, lax.div(other, NV), lax.rem(other, NV)),
        )

    def t_copy(g, o, slot):
        x, y = lax.div(tex, 4), lax.rem(tex, 4)
        other = 4 * lax.rem(x + o // 4, 4) + lax.rem(y + o % 4, 4)
        return remote(
            part.at[g], t_land.at[g, slot(other)], t_send.at[g, o], t_recv.at[g, slot(other)], (other, i, j)
        )

    def last_copy(g, o, slot):
        other = lax.rem((i, j)[g] + o, 4)
        device = (tex, other, j) if g == 0 else (tex, i, other)
        return remote(
            whole.at[g], last_land.at[g, slot(other)], last_send.at[g, o], last_recv.at[g, slot(other)], device
        )

    def start_all(copy, g, order, own):
        for o in order:
            copy(g, o, lambda other: own).start()

    def wait_all(copy, g, order):
        for o in order:
            copy(g, o, lambda other: other).wait_recv()

    z_order = (8, 7, 9, 6, 10, 5, 11, 4, 12, 3, 13, 2, 14, 1, 15)
    t_order = (10, 9, 11, 6, 14, 8, 2, 5, 7, 13, 15, 4, 12, 1, 3)

    def z_start(g, total):
        pages[g] = to_pages(total, g == 0)
        start_all(z_copy, g, z_order, me)
        z_land[g, me] = pages[g, me]

    def z_end_t_start(g):
        wait_all(z_copy, g, z_order)
        part[g] = jnp.sum(z_land[g], axis=0)
        start_all(t_copy, g, t_order, tex)
        t_land[g, tex] = part[g]

    def t_end_last_start(g):
        wait_all(t_copy, g, t_order)
        whole[g] = jnp.sum(t_land[g], axis=0)
        start_all(last_copy, g, (2, 1, 3), (i, j)[g])
        last_land[g, (i, j)[g]] = whole[g]

    def last_end(g, out, scale):
        wait_all(last_copy, g, (2, 1, 3))
        for q in range(4):
            out[5 * q : 5 * q + 5, :] = last_land[g, q, 0:5, 0:80] * scale

    z_start(0, products(
        jnp.concatenate([share[h, s * ROWS + g * GROUP : s * ROWS + (g + 1) * GROUP, :] for s in range(NV)], axis=0)
        for h in range(2)
        for g in range(ROWS // GROUP)
    ))

    for h in range(2):
        for o in (2, 3, 1):
            core_copy(h, o, j, mine).start()
        pltpu.make_async_copy(
            pieces.at[h, piece_of(j), :], core_land.at[2 * mine + h], core_recv.at[h, j]
        ).start()

    def light_products(h):
        for k in range(NL):
            pltpu.make_async_copy(pieces.at[h, pl.ds(0, PIECE), :], light_land.at[h, k], light_recv.at[h, k]).wait()
        return products(
            jnp.concatenate([light_land[h, k, g * GROUP : (g + 1) * GROUP, :] for k in range(NL)], axis=0)
            for g in range(PIECE // GROUP)
        )

    first = light_products(0)
    z_end_t_start(0)
    z_start(1, first + light_products(1))
    t_end_last_start(0)
    z_end_t_start(1)
    for h in range(2):
        pltpu.make_async_copy(
            pieces.at[h, piece_of(j), :], core_land.at[2 * mine + h], core_recv.at[h, j]
        ).wait()
        for o in (1, 2, 3):
            core_copy(h, o, others[o], shares[o]).wait_recv()
    for n in range(2 * NV):
        core_ref[:, n * HB : (n + 1) * HB] = core_land[n]
    last_end(0, view_ref, view_scale)
    t_end_last_start(1)
    last_end(1, light_ref, light_scale)

    for o in (1, 2, 3):
        basis_copy(o, j).wait_send()
        for h in range(2):
            slab_copy(h, o, j).wait_send()
            core_copy(h, o, j, mine).wait_send()
    for o in range(NV):
        ci, cj = centers[o]

        @pl.when(jnp.logical_not(jnp.logical_and(ci == i, cj == j)))
        def _():
            for h in range(2):
                light_copy(h, o, ci, cj).wait_send()

    for g in range(2):
        for o in z_order:
            z_copy(g, o, lambda other: me).wait_send()
        for o in t_order:
            t_copy(g, o, lambda other: tex).wait_send()
        for o in (2, 1, 3):
            last_copy(g, o, lambda other: (i, j)[g]).wait_send()


def body(slab, basis):
    texels = lax.axis_size("texel")
    columns_all = slab.shape[2] * texels
    view_scale = 1.0 / (LB * NL * columns_all)
    light_scale = 1.0 / (RB * NV * columns_all)
    hbm = pl.BlockSpec(memory_space=pltpu.HBM)
    vmem = pl.BlockSpec(memory_space=pltpu.VMEM)
    dma = pltpu.SemaphoreType.DMA
    view_gram, core, light_gram = pl.pallas_call(
        functools.partial(kernel, view_scale, light_scale),
        out_shape=(
            pltpu.VMEM((VB, 80), F32),
            pltpu.VMEM((PIECE, 4 * CB), BF),
            pltpu.VMEM((LB, 80), F32),
        ),
        in_specs=[hbm] * 2,
        out_specs=(vmem,) * 3,
        scratch_shapes=[
            pltpu.VMEM(slab.shape, BF),
            pltpu.VMEM(basis.shape, BF),
            pltpu.VMEM((GROUP, NV * ROWS), BF),
            pltpu.VMEM((2 * NV, ROWS, HB), BF),
            pltpu.VMEM((2, NV * ROWS, HB), BF),
            pltpu.VMEM((32, 128), BF),
            pltpu.VMEM((NV, 32, 128), BF),
            pltpu.VMEM((NV * PIECE, NV * ROWS), BF),
            pltpu.VMEM((2, NV * PIECE, HB), BF),
            pltpu.VMEM((2 * NV, PIECE, HB), BF),
            pltpu.VMEM((2, NL, PIECE, HB), BF),
            pltpu.VMEM((2, PAGES, 8, 128), F32),
            pltpu.VMEM((2, PAGES, 8, 128), F32),
            pltpu.VMEM((2, 8, 128), F32),
            pltpu.VMEM((2, texels, 8, 128), F32),
            pltpu.VMEM((2, 8, 128), F32),
            pltpu.VMEM((2, 4, 8, 128), F32),
            dma((2,)), dma((NV,)), dma((NV,)), dma((2, NV)), dma((2, NV)), dma((2, NV)), dma((2, NV)),
            dma((2, NV)), dma((2, NL)), dma((2, PAGES)), dma((2, PAGES)), dma((2, texels)), dma((2, texels)),
            dma((2, 4)), dma((2, 4)),
        ],
        compiler_params=pltpu.CompilerParams(
            collective_id=0, has_side_effects=True, vmem_limit_bytes=40 * 1024 * 1024
        ),
    )(pltpu.with_memory_space_constraint(slab, pltpu.HBM), pltpu.with_memory_space_constraint(basis, pltpu.HBM))
    return view_gram, core.reshape(RB, LB, 4 * CB), light_gram


def solution(mesh):
    return jax.shard_map(
        body,
        mesh=mesh,
        in_specs=(P("light", "view", "texel"), P("view", None)),
        out_specs=(P("view", None), P("view", "light", "texel"), P("light", None)),
        check_vma=False,
    )
```

```python
import jax
import jax.numpy as jnp
from jax import lax
from jax.experimental import pallas as pl
from jax.experimental.pallas import tpu as pltpu
from jax.sharding import PartitionSpec as P

MESH = pl.DeviceIdType.MESH
BF = jnp.bfloat16
F32 = jnp.float32
LB = 20
VB = 20
NV = 4
NL = 4
RB = 12
CB = 256
ROWS = LB * VB
PIECE = RB * LB
NG = 5
GROUP = 4 * VB
STACK = NV * GROUP
AHEAD = 3
PART = 4 * RB
PAGES = NL * NV


def cells(shape):
    return lax.broadcasted_iota(jnp.int32, shape, 0), lax.broadcasted_iota(jnp.int32, shape, 1)


def div20(x):
    return (x * 3277) >> 16


def ones_where(condition, dtype=BF):
    return jnp.where(condition, 1.0, 0.0).astype(dtype)


def expand_table():
    row, col = cells((NV * 32, STACK))
    line = div20(col)
    return ones_where(row == 32 * (line >> 2) + col - VB * line)


def spread_table():
    row, col = cells((NV * PART, 128))
    return ones_where((row >> 2) == col)


def light_mask():
    row, col = cells((NV * PART, STACK))
    return ones_where((row & 3) == (div20(col) & 3))


def order_table():
    row, col = cells((PIECE, PIECE))
    group = (col * 1366) >> 16
    rest = col - PART * group
    return ones_where(row == LB * (rest >> 2) + 4 * group + (rest & 3))


def gram_place(g, x):
    if g:
        return 4 * (x >> 4) + (x & 3), (x >> 2) & 3
    line = div20(x)
    return 20 * (line >> 2) + x - 20 * line, line & 3


def keep_table(g):
    row, col = cells((STACK, STACK))
    return ones_where(gram_place(g, row)[1] == gram_place(g, col)[1], F32)


def pick_table(g):
    row, col = cells((8 * PAGES, STACK))
    p, q = row >> 3, row & 7
    if g == 0:
        p = NL * (p & 3) + (p >> 2)
    return ones_where((q < 5) & (5 * p + q == gram_place(g, col)[0]))


def gather_table(g):
    row, col = cells((STACK, 128))
    return ones_where(gram_place(g, row)[0] == col)


def odd_share(k, t):
    return lax.rem(lax.div(k + 1 - t, 2), 2)


def share_of(k, j):
    e, t = lax.div(j, 2), lax.rem(j, 2)
    return 2 * t + lax.rem(odd_share(k, t) + 1 - e, 2)


def member_for(k, b):
    t, u = lax.div(b, 2), lax.rem(b, 2)
    return 2 * lax.rem(odd_share(k, t) + 1 + u, 2) + t


def center_of(b, n):
    t, u = lax.div(b, 2), lax.rem(b, 2)
    z = lax.rem(1 + 4 * u + 2 * t + lax.div(n, 2), 8)
    return lax.div(z, 2), 2 * lax.rem(z, 2) + lax.rem(n, 2)


def split_dot(a, b):
    def parts(x):
        hi = x.astype(BF)
        return hi, (x - hi.astype(F32)).astype(BF)

    if a.dtype == BF:
        return sum(jnp.dot(a, p, preferred_element_type=F32) for p in parts(b))
    return sum(jnp.dot(p, b, preferred_element_type=F32) for p in parts(a))


def remote(src, dst, send, recv, device):
    return pltpu.make_async_remote_copy(
        src_ref=src, dst_ref=dst, send_sem=send, recv_sem=recv, device_id=device, device_id_type=MESH
    )


def kernel(
    slab_hbm, basis_hbm,
    gram_ref, core_ref,
    slab_ref, basis_ref, keep_ref, pick_ref, gather_ref, order_ref, weights,
    dense, share, own_basis, all_basis, pieces, core_land, light_land,
    pages, z_land, part, t_land, whole, last_land,
    load, basis_send, basis_recv, slab_send, slab_recv, core_send, core_recv,
    light_send, light_recv, z_send, z_recv, t_send, t_recv, last_send, last_recv,
):
    texels = lax.axis_size("texel")
    tex, i, j = lax.axis_index("texel"), lax.axis_index("light"), lax.axis_index("view")
    me = i * NV + j
    mine = share_of(i, j)

    load_basis = pltpu.make_async_copy(basis_hbm, basis_ref, load.at[NG])
    load_basis.start()
    load_slab = [
        pltpu.make_async_copy(slab_hbm.at[4 * g : 4 * g + 4], slab_ref.at[4 * g : 4 * g + 4], load.at[g])
        for g in range(NG)
    ]
    for copy in load_slab:
        copy.start()
    barrier = pltpu.get_barrier_semaphore()

    def greet_z(o, c):
        other = lax.rem(me + o, PAGES)
        pl.semaphore_signal(
            barrier, inc=1, device_id=(tex, lax.div(other, NV), lax.rem(other, NV)), device_id_type=MESH
        )
        return c

    def greet_t(o, c):
        pl.semaphore_signal(barrier, inc=1, device_id=(lax.rem(tex + o, texels), i, j), device_id_type=MESH)
        return c

    lax.fori_loop(1, PAGES, greet_z, 0)
    lax.fori_loop(1, texels, greet_t, 0)

    own_basis[...] = jnp.zeros_like(own_basis)
    load_basis.wait()
    own_basis[0:VB, 0 : NV * RB] = basis_ref[...]

    def lay_out(g):
        load_slab[g].wait()
        for n in range(NV):
            for l in range(4 * g, 4 * g + 4):
                dense[n, l * VB : (l + 1) * VB, :] = slab_ref[l, :, n * CB : (n + 1) * CB]

    lay_out(0)
    pl.semaphore_wait(barrier, PAGES - 1 + texels - 1)

    others = [lax.rem(j + o, NV) for o in range(NV)]
    shares = [share_of(i, other) for other in others]

    def rows_of(g):
        return pl.ds(g * GROUP, GROUP)

    def part_of(p):
        return pl.ds(pl.multiple_of(p * PART, 16), PART)

    def slab_copy(g, o, slot):
        return remote(
            dense.at[shares[o], rows_of(g), :], share.at[slot, rows_of(g), :], slab_send.at[g, o],
            slab_recv.at[g, slot], (tex, i, others[o]),
        )

    def basis_copy(o, slot):
        return remote(own_basis, all_basis.at[slot], basis_send.at[o], basis_recv.at[slot], (tex, i, others[o]))

    for o in (2, 3, 1):
        basis_copy(o, j).start()
    local = [
        pltpu.make_async_copy(dense.at[mine, rows_of(g), :], share.at[j, rows_of(g), :], slab_recv.at[g, j])
        for g in range(NG)
    ]

    def slab_start(g):
        for o in (2, 3, 1):
            slab_copy(g, o, j).start()
        local[g].start()

    for g in range(NG):
        if g:
            lay_out(g)
        if g < AHEAD:
            slab_start(g)
    all_basis[j] = own_basis[...]
    spread, expand, mask = spread_table(), expand_table(), light_mask()
    for o in (1, 2, 3):
        basis_copy(o, others[o]).wait_recv()

    table = lax.dot_general(
        all_basis[...].reshape(NV * 32, 128), expand, (((0,), (0,)), ((), ())), preferred_element_type=F32
    ).astype(BF)
    weights[...] = jnp.dot(spread, table, preferred_element_type=F32).astype(BF) * mask

    ahead = lax.rem(1 + 4 * lax.rem(mine, 2) + 2 * lax.div(mine, 2) - 2 * i - lax.div(j, 2) + 8, 8)
    far = 1 - lax.div(ahead, 4)
    turns = [2 * far, 2 * far + 1, 2 * (1 - far), 2 * (1 - far) + 1]
    centers = [center_of(mine, p) for p in turns]

    def light_copy(g, o, ci, cj):
        return remote(
            pieces.at[g, part_of(turns[o]), :], light_land.at[i, g], light_send.at[g, o], light_recv.at[g, i],
            (tex, ci, cj),
        )

    def core_copy(o, slot, place):
        return remote(
            pieces.at[:, part_of(others[o]), :], core_land.at[place], core_send.at[o], core_recv.at[slot],
            (tex, i, others[o]),
        )

    def stack_of(g):
        return jnp.concatenate([share[s, g * GROUP : (g + 1) * GROUP, :] for s in range(NV)], axis=0)

    for g in range(NG):
        local[g].wait()
        for o in (1, 2, 3):
            slab_copy(g, o, others[o]).wait_recv()
        if g + AHEAD < NG:
            slab_start(g + AHEAD)
        pieces[g] = jnp.dot(weights[...], stack_of(g), preferred_element_type=F32).astype(BF)
        for o in range(NV):
            ci, cj = centers[o]
            here = jnp.logical_and(ci == i, cj == j)

            @pl.when(here)
            def _():
                pltpu.make_async_copy(
                    pieces.at[g, part_of(turns[o]), :], light_land.at[i, g], light_recv.at[g, i]
                ).start()

            @pl.when(jnp.logical_not(here))
            def _():
                light_copy(g, o, ci, cj).start()

    def products(stacks):
        wide = jnp.concatenate(list(stacks), axis=1)
        return lax.dot_general(wide, wide, (((1,), (1,)), ((), ())), preferred_element_type=F32)

    def to_pages(g, total):
        rows = split_dot(pick_ref[g], total * keep_ref[g])
        return split_dot(rows, gather_ref[g]).reshape(PAGES, 8, 128)

    def z_copy(g, o, slot):
        other = lax.rem(me + o, PAGES)
        return remote(
            pages.at[g, other], z_land.at[g, slot(other)], z_send.at[g, o], z_recv.at[g, slot(other)],
            (tex, lax.div(other, NV), lax.rem(other, NV)),
        )

    def t_copy(g, o, slot):
        x, y = lax.div(tex, 4), lax.rem(tex, 4)
        other = 4 * lax.rem(x + o // 4, 4) + lax.rem(y + o % 4, 4)
        return remote(
            part.at[g], t_land.at[g, slot(other)], t_send.at[g, o], t_recv.at[g, slot(other)], (other, i, j)
        )

    def last_copy(g, o, slot):
        other = lax.rem((i, j)[g] + o, 4)
        device = (tex, other, j) if g == 0 else (tex, i, other)
        return remote(
            whole.at[g], last_land.at[g, slot(other)], last_send.at[g, o], last_recv.at[g, slot(other)], device
        )

    def start_all(copy, g, order, own):
        for o in order:
            copy(g, o, lambda other: own).start()

    def wait_all(copy, g, order):
        for o in order:
            copy(g, o, lambda other: other).wait_recv()

    z_order = (8, 7, 9, 6, 10, 5, 11, 4, 12, 3, 13, 2, 14, 1, 15)
    t_order = (10, 9, 11, 6, 14, 8, 2, 5, 7, 13, 15, 4, 12, 1, 3)

    def z_start(g, total):
        pages[g] = to_pages(g, total)
        start_all(z_copy, g, z_order, me)
        z_land[g, me] = pages[g, me]

    def z_end_t_start(g):
        wait_all(z_copy, g, z_order)
        part[g] = jnp.sum(z_land[g], axis=0)
        start_all(t_copy, g, t_order, tex)
        t_land[g, tex] = part[g]

    def t_end_last_start(g):
        wait_all(t_copy, g, t_order)
        whole[g] = jnp.sum(t_land[g], axis=0)
        start_all(last_copy, g, (2, 1, 3), (i, j)[g])
        last_land[g, (i, j)[g]] = whole[g]

    def last_end(g):
        wait_all(last_copy, g, (2, 1, 3))
        for q in range(4):
            gram_ref[g, 5 * q : 5 * q + 5, :] = last_land[g, q, 0:5, 0:80]

    for g in range(2):
        keep_ref[g] = keep_table(g)
        pick_ref[g] = pick_table(g)
        gather_ref[g] = gather_table(g)
    z_start(0, products(stack_of(g) for g in range(NG)))

    for o in (2, 3, 1):
        core_copy(o, j, mine).start()
    own_piece = pltpu.make_async_copy(pieces.at[:, part_of(j), :], core_land.at[mine], core_recv.at[j])
    own_piece.start()
    order_ref[...] = order_table()

    for g in range(NG):
        for k in range(NL):
            pltpu.make_async_copy(pieces.at[g, part_of(0), :], light_land.at[k, g], light_recv.at[g, k]).wait()
    z_start(1, products(
        jnp.concatenate(
            [light_land[k, g, 16 * m : 16 * m + 16, :] for k in range(NL) for g in range(NG)], axis=0
        )
        for m in range(PART // 16)
    ))
    z_end_t_start(0)
    for o in (1, 2, 3):
        basis_copy(o, j).wait_send()
        for g in range(NG):
            slab_copy(g, o, j).wait_send()
    for o in range(NV):
        ci, cj = centers[o]

        @pl.when(jnp.logical_not(jnp.logical_and(ci == i, cj == j)))
        def _():
            for g in range(NG):
                light_copy(g, o, ci, cj).wait_send()

    z_end_t_start(1)
    t_end_last_start(0)
    own_piece.wait()
    for o in (1, 2, 3):
        core_copy(o, others[o], shares[o]).wait_recv()
    for n in range(NV):
        core_ref[:, n * CB : (n + 1) * CB] = jnp.dot(
            order_ref[...], core_land[n].reshape(PIECE, CB), preferred_element_type=F32
        ).astype(BF)
    for o in (1, 2, 3):
        core_copy(o, j, mine).wait_send()
    for o in t_order:
        t_copy(0, o, lambda other: tex).wait_send()
    for g in range(2):
        for o in z_order:
            z_copy(g, o, lambda other: me).wait_send()
    t_end_last_start(1)
    for o in t_order:
        t_copy(1, o, lambda other: tex).wait_send()
    last_end(0)
    last_end(1)

    for g in range(2):
        for o in (2, 1, 3):
            last_copy(g, o, lambda other: (i, j)[g]).wait_send()


def body(slab, basis):
    texels = lax.axis_size("texel")
    columns_all = slab.shape[2] * texels
    view_scale = 1.0 / (LB * NL * columns_all)
    light_scale = 1.0 / (RB * NV * columns_all)
    hbm = pl.BlockSpec(memory_space=pltpu.HBM)
    vmem = pl.BlockSpec(memory_space=pltpu.VMEM)
    dma = pltpu.SemaphoreType.DMA
    grams, core = pl.pallas_call(
        kernel,
        out_shape=(
            pltpu.VMEM((2, VB, 80), F32),
            pltpu.VMEM((PIECE, 4 * CB), BF),
        ),
        in_specs=[hbm] * 2,
        out_specs=(vmem,) * 2,
        scratch_shapes=[
            pltpu.VMEM(slab.shape, BF),
            pltpu.VMEM(basis.shape, BF),
            pltpu.VMEM((2, STACK, STACK), F32),
            pltpu.VMEM((2, 8 * PAGES, STACK), BF),
            pltpu.VMEM((2, STACK, 128), BF),
            pltpu.VMEM((PIECE, PIECE), BF),
            pltpu.VMEM((NV * PART, STACK), BF),
            pltpu.VMEM((NV, ROWS, CB), BF),
            pltpu.VMEM((NV, ROWS, CB), BF),
            pltpu.VMEM((32, 128), BF),
            pltpu.VMEM((NV, 32, 128), BF),
            pltpu.VMEM((NG, NV * PART, CB), BF),
            pltpu.VMEM((NV, NG, PART, CB), BF),
            pltpu.VMEM((NL, NG, PART, CB), BF),
            pltpu.VMEM((2, PAGES, 8, 128), F32),
            pltpu.VMEM((2, PAGES, 8, 128), F32),
            pltpu.VMEM((2, 8, 128), F32),
            pltpu.VMEM((2, texels, 8, 128), F32),
            pltpu.VMEM((2, 8, 128), F32),
            pltpu.VMEM((2, 4, 8, 128), F32),
            dma((NG + 1,)), dma((NV,)), dma((NV,)), dma((NG, NV)), dma((NG, NV)), dma((NV,)), dma((NV,)),
            dma((NG, NV)), dma((NG, NL)), dma((2, PAGES)), dma((2, PAGES)), dma((2, texels)), dma((2, texels)),
            dma((2, 4)), dma((2, 4)),
        ],
        compiler_params=pltpu.CompilerParams(
            collective_id=0, has_side_effects=True, vmem_limit_bytes=40 * 1024 * 1024
        ),
    )(pltpu.with_memory_space_constraint(slab, pltpu.HBM), pltpu.with_memory_space_constraint(basis, pltpu.HBM))
    return grams[0] * view_scale, core.reshape(RB, LB, 4 * CB), grams[1] * light_scale


def solution(mesh):
    return jax.shard_map(
        body,
        mesh=mesh,
        in_specs=(P("light", "view", "texel"), P("view", None)),
        out_specs=(P("view", None), P("view", "light", "texel"), P("light", None)),
        check_vma=False,
    )
```

```python
import jax
import jax.numpy as jnp
from jax import lax
from jax.experimental import pallas as pl
from jax.experimental.pallas import tpu as pltpu
from jax.sharding import PartitionSpec as P

MESH = pl.DeviceIdType.MESH
BF = jnp.bfloat16
F32 = jnp.float32
LB = 20
VB = 20
NV = 4
NL = 4
RB = 12
CB = 256
ROWS = LB * VB
PIECE = RB * LB
NG = 5
GROUP = 4 * VB
STACK = NV * GROUP
AHEAD = 3
PART = 4 * RB
PAGES = NL * NV


def cells(shape):
    return lax.broadcasted_iota(jnp.int32, shape, 0), lax.broadcasted_iota(jnp.int32, shape, 1)


def div20(x):
    return (x * 3277) >> 16


def ones_where(condition, dtype=BF):
    return jnp.where(condition, 1.0, 0.0).astype(dtype)


def expand_table():
    row, col = cells((NV * 32, STACK))
    line = div20(col)
    return ones_where(row == 32 * (line >> 2) + col - VB * line)


def spread_table():
    row, col = cells((NV * PART, 128))
    return ones_where((row >> 2) == col)


def light_mask():
    row, col = cells((NV * PART, STACK))
    return ones_where((row & 3) == (div20(col) & 3))


def order_table():
    row, col = cells((PIECE, PIECE))
    group = (col * 1366) >> 16
    rest = col - PART * group
    return ones_where(row == LB * (rest >> 2) + 4 * group + (rest & 3))


def gram_place(g, x):
    if g:
        return 4 * (x >> 4) + (x & 3), (x >> 2) & 3
    line = div20(x)
    return 20 * (line >> 2) + x - 20 * line, line & 3


def keep_table(g):
    row, col = cells((STACK, STACK))
    return ones_where(gram_place(g, row)[1] == gram_place(g, col)[1], F32)


def pick_table(g):
    row, col = cells((8 * PAGES, STACK))
    p, q = row >> 3, row & 7
    return ones_where((q < 5) & (5 * p + q == gram_place(g, col)[0]))


def gather_table(g):
    row, col = cells((STACK, 128))
    return ones_where(gram_place(g, row)[0] == col)


def odd_share(k, t):
    return lax.rem(lax.div(k + 1 - t, 2), 2)


def share_of(k, j):
    e, t = lax.div(j, 2), lax.rem(j, 2)
    return 2 * t + lax.rem(odd_share(k, t) + 1 - e, 2)


def member_for(k, b):
    t, u = lax.div(b, 2), lax.rem(b, 2)
    return 2 * lax.rem(odd_share(k, t) + 1 + u, 2) + t


def center_of(b, n):
    t, u = lax.div(b, 2), lax.rem(b, 2)
    z = lax.rem(1 + 4 * u + 2 * t + lax.div(n, 2), 8)
    return lax.div(z, 2), 2 * lax.rem(z, 2) + lax.rem(n, 2)


def split_dot(a, b):
    def parts(x):
        hi = x.astype(BF)
        return hi, (x - hi.astype(F32)).astype(BF)

    if a.dtype == BF:
        return sum(jnp.dot(a, p, preferred_element_type=F32) for p in parts(b))
    return sum(jnp.dot(p, b, preferred_element_type=F32) for p in parts(a))


def remote(src, dst, send, recv, device):
    return pltpu.make_async_remote_copy(
        src_ref=src, dst_ref=dst, send_sem=send, recv_sem=recv, device_id=device, device_id_type=MESH
    )


def kernel(
    slab_hbm, basis_hbm,
    gram_ref, core_ref,
    slab_ref, basis_ref, keep_ref, pick_ref, gather_ref, order_ref, weights,
    dense, share, own_basis, all_basis, pieces, core_land, light_land,
    pages, z_land, part, t_land, whole, last_land,
    load, basis_send, basis_recv, slab_send, slab_recv, core_send, core_recv,
    light_send, light_recv, z_send, z_recv, t_send, t_recv, last_send, last_recv, vz_send, vlast_send,
):
    texels = lax.axis_size("texel")
    tex, i, j = lax.axis_index("texel"), lax.axis_index("light"), lax.axis_index("view")
    me = i * NV + j
    mine = share_of(i, j)

    load_basis = pltpu.make_async_copy(basis_hbm, basis_ref, load.at[NG])
    load_basis.start()
    load_slab = [
        pltpu.make_async_copy(slab_hbm.at[4 * g : 4 * g + 4], slab_ref.at[4 * g : 4 * g + 4], load.at[g])
        for g in range(NG)
    ]
    for copy in load_slab:
        copy.start()
    barrier = pltpu.get_barrier_semaphore()

    def greet_z(o, c):
        other = lax.rem(me + o, PAGES)
        pl.semaphore_signal(
            barrier, inc=1, device_id=(tex, lax.div(other, NV), lax.rem(other, NV)), device_id_type=MESH
        )
        return c

    def greet_t(o, c):
        pl.semaphore_signal(barrier, inc=1, device_id=(lax.rem(tex + o, texels), i, j), device_id_type=MESH)
        return c

    lax.fori_loop(1, PAGES, greet_z, 0)
    lax.fori_loop(1, texels, greet_t, 0)

    own_basis[...] = jnp.zeros_like(own_basis)
    load_basis.wait()
    own_basis[0:VB, 0 : NV * RB] = basis_ref[...]

    def lay_out(g):
        load_slab[g].wait()
        for n in range(NV):
            for l in range(4 * g, 4 * g + 4):
                dense[n, l * VB : (l + 1) * VB, :] = slab_ref[l, :, n * CB : (n + 1) * CB]

    lay_out(0)
    pl.semaphore_wait(barrier, PAGES - 1 + texels - 1)

    others = [lax.rem(j + o, NV) for o in range(NV)]
    shares = [share_of(i, other) for other in others]

    def rows_of(g):
        return pl.ds(g * GROUP, GROUP)

    def part_of(p):
        return pl.ds(pl.multiple_of(p * PART, 16), PART)

    def slab_copy(g, o, slot):
        return remote(
            dense.at[shares[o], rows_of(g), :], share.at[slot, rows_of(g), :], slab_send.at[g, o],
            slab_recv.at[g, slot], (tex, i, others[o]),
        )

    def basis_copy(o, slot):
        return remote(own_basis, all_basis.at[slot], basis_send.at[o], basis_recv.at[slot], (tex, i, others[o]))

    for o in (2, 3, 1):
        basis_copy(o, j).start()
    local = [
        pltpu.make_async_copy(dense.at[mine, rows_of(g), :], share.at[j, rows_of(g), :], slab_recv.at[g, j])
        for g in range(NG)
    ]

    def slab_start(g):
        for o in (2, 3, 1):
            slab_copy(g, o, j).start()
        local[g].start()

    for g in range(NG):
        if g:
            lay_out(g)
        if g < AHEAD:
            slab_start(g)
    all_basis[j] = own_basis[...]
    spread, expand, mask = spread_table(), expand_table(), light_mask()
    for o in (1, 2, 3):
        basis_copy(o, others[o]).wait_recv()

    table = lax.dot_general(
        all_basis[...].reshape(NV * 32, 128), expand, (((0,), (0,)), ((), ())), preferred_element_type=F32
    ).astype(BF)
    weights[...] = jnp.dot(spread, table, preferred_element_type=F32).astype(BF) * mask

    ahead = lax.rem(1 + 4 * lax.rem(mine, 2) + 2 * lax.div(mine, 2) - 2 * i - lax.div(j, 2) + 8, 8)
    far = 1 - lax.div(ahead, 4)
    turns = [2 * far, 2 * far + 1, 2 * (1 - far), 2 * (1 - far) + 1]
    centers = [center_of(mine, p) for p in turns]

    def light_copy(g, o, ci, cj):
        return remote(
            pieces.at[g, part_of(turns[o]), :], light_land.at[i, g], light_send.at[g, o], light_recv.at[g, i],
            (tex, ci, cj),
        )

    def core_copy(o, slot, place):
        return remote(
            pieces.at[:, part_of(others[o]), :], core_land.at[place], core_send.at[o], core_recv.at[slot],
            (tex, i, others[o]),
        )

    def stack_of(g):
        return jnp.concatenate([share[s, g * GROUP : (g + 1) * GROUP, :] for s in range(NV)], axis=0)

    for g in range(NG):
        local[g].wait()
        for o in (1, 2, 3):
            slab_copy(g, o, others[o]).wait_recv()
        if g + AHEAD < NG:
            slab_start(g + AHEAD)
        pieces[g] = jnp.dot(weights[...], stack_of(g), preferred_element_type=F32).astype(BF)
        for o in range(NV):
            ci, cj = centers[o]
            here = jnp.logical_and(ci == i, cj == j)

            @pl.when(here)
            def _():
                pltpu.make_async_copy(
                    pieces.at[g, part_of(turns[o]), :], light_land.at[i, g], light_recv.at[g, i]
                ).start()

            @pl.when(jnp.logical_not(here))
            def _():
                light_copy(g, o, ci, cj).start()

    def products(stacks):
        wide = jnp.concatenate(list(stacks), axis=1)
        return lax.dot_general(wide, wide, (((1,), (1,)), ((), ())), preferred_element_type=F32)

    def to_pages(g, total):
        rows = split_dot(pick_ref[g], total * keep_ref[g])
        return split_dot(rows, gather_ref[g]).reshape(PAGES, 8, 128)

    x, y = lax.div(tex, 4), lax.rem(tex, 4)

    def texel_at(o):
        return 4 * lax.rem(x + o // 4, 4) + lax.rem(y + o % 4, 4)

    def z_copy(o, slot):
        other = lax.rem(me + o, PAGES)
        return remote(
            pages.at[1, other], z_land.at[1, slot(other)], z_send.at[o], z_recv.at[1, slot(other)],
            (tex, lax.div(other, NV), lax.rem(other, NV)),
        )

    def t_copy(o, slot):
        other = texel_at(o)
        return remote(
            part.at[1], t_land.at[1, slot(other)], t_send.at[1, o], t_recv.at[1, slot(other)], (other, i, j)
        )

    def last_copy(o, slot):
        other = lax.rem(j + o, NV)
        return remote(
            whole.at[1], last_land.at[1, slot(other)], last_send.at[o], last_recv.at[1, slot(other)], (tex, i, other)
        )

    takes = j == x

    def vt_copy(o, slot):
        other = texel_at(o)
        return remote(
            pages.at[0, other], t_land.at[0, slot(other)], t_send.at[0, o], t_recv.at[0, slot(other)], (other, i, j)
        )

    def vz_copy(o, slot):
        return remote(
            part.at[0], z_land.at[0, slot], vz_send.at[o], z_recv.at[0, slot], (tex, lax.rem(i + o, NL), x)
        )

    def vlast_copy(o, slot):
        return remote(
            whole.at[0], last_land.at[0, slot], vlast_send.at[o], last_recv.at[0, slot], (texel_at(o), i, j)
        )

    def start_all(copy, order, own):
        for o in order:
            copy(o, lambda other: own).start()

    def wait_all(copy, order):
        for o in order:
            copy(o, lambda other: other).wait_recv()

    def sent_all(copy, order, own):
        for o in order:
            copy(o, lambda other: own).wait_send()

    z_order = (8, 7, 9, 6, 10, 5, 11, 4, 12, 3, 13, 2, 14, 1, 15)
    t_order = (10, 9, 11, 6, 14, 8, 2, 5, 7, 13, 15, 4, 12, 1, 3)

    for g in range(2):
        keep_ref[g] = keep_table(g)
        pick_ref[g] = pick_table(g)
        gather_ref[g] = gather_table(g)
    pages[0] = to_pages(0, products(stack_of(g) for g in range(NG)))
    start_all(vt_copy, t_order, tex)
    t_land[0, tex] = pages[0, tex]

    for o in (2, 3, 1):
        core_copy(o, j, mine).start()
    own_piece = pltpu.make_async_copy(pieces.at[:, part_of(j), :], core_land.at[mine], core_recv.at[j])
    own_piece.start()
    order_ref[...] = order_table()

    for g in range(NG):
        for k in range(NL):
            pltpu.make_async_copy(pieces.at[g, part_of(0), :], light_land.at[k, g], light_recv.at[g, k]).wait()
    pages[1] = to_pages(1, products(
        jnp.concatenate(
            [light_land[k, g, 16 * m : 16 * m + 16, :] for k in range(NL) for g in range(NG)], axis=0
        )
        for m in range(PART // 16)
    ))
    start_all(z_copy, z_order, me)
    z_land[1, me] = pages[1, me]

    wait_all(vt_copy, t_order)
    part[0] = jnp.sum(t_land[0], axis=0)
    for o in (2, 1, 3):
        vz_copy(o, me).start()

    @pl.when(takes)
    def _():
        z_land[0, me] = part[0]

    @pl.when(jnp.logical_not(takes))
    def _():
        vz_copy(0, me).start()

    for o in (1, 2, 3):
        basis_copy(o, j).wait_send()
        for g in range(NG):
            slab_copy(g, o, j).wait_send()
    for o in range(NV):
        ci, cj = centers[o]

        @pl.when(jnp.logical_not(jnp.logical_and(ci == i, cj == j)))
        def _():
            for g in range(NG):
                light_copy(g, o, ci, cj).wait_send()

    sent_all(vt_copy, t_order, tex)
    wait_all(z_copy, z_order)
    part[1] = jnp.sum(z_land[1], axis=0)
    start_all(t_copy, t_order, tex)
    t_land[1, tex] = part[1]

    @pl.when(takes)
    def _():
        for o in z_order:
            vz_copy(0, lax.rem(me + o, PAGES)).wait_recv()
        whole[0] = jnp.sum(z_land[0], axis=0)
        for o in t_order:
            vlast_copy(o, y).start()
        last_land[0, y] = whole[0]

    own_piece.wait()
    for o in (1, 2, 3):
        core_copy(o, others[o], shares[o]).wait_recv()
    for n in range(NV):
        core_ref[:, n * CB : (n + 1) * CB] = jnp.dot(
            order_ref[...], core_land[n].reshape(PIECE, CB), preferred_element_type=F32
        ).astype(BF)
    for o in (1, 2, 3):
        core_copy(o, j, mine).wait_send()
        vz_copy(o, me).wait_send()

    @pl.when(jnp.logical_not(takes))
    def _():
        vz_copy(0, me).wait_send()

    sent_all(z_copy, z_order, me)
    wait_all(t_copy, t_order)
    whole[1] = jnp.sum(t_land[1], axis=0)
    start_all(last_copy, (2, 1, 3), j)
    last_land[1, j] = whole[1]

    for q in range(4):
        @pl.when(jnp.logical_not(jnp.logical_and(takes, y == q)))
        def _():
            vlast_copy(1, q).wait_recv()

    @pl.when(takes)
    def _():
        for o in t_order:
            vlast_copy(o, y).wait_send()

    sent_all(t_copy, t_order, tex)
    wait_all(last_copy, (2, 1, 3))
    for g in range(2):
        for q in range(4):
            gram_ref[g, 5 * q : 5 * q + 5, :] = last_land[g, q, 0:5, 0:80]
    sent_all(last_copy, (2, 1, 3), j)


def body(slab, basis):
    texels = lax.axis_size("texel")
    columns_all = slab.shape[2] * texels
    view_scale = 1.0 / (LB * NL * columns_all)
    light_scale = 1.0 / (RB * NV * columns_all)
    hbm = pl.BlockSpec(memory_space=pltpu.HBM)
    vmem = pl.BlockSpec(memory_space=pltpu.VMEM)
    dma = pltpu.SemaphoreType.DMA
    grams, core = pl.pallas_call(
        kernel,
        out_shape=(
            pltpu.VMEM((2, VB, 80), F32),
            pltpu.VMEM((PIECE, 4 * CB), BF),
        ),
        in_specs=[hbm] * 2,
        out_specs=(vmem,) * 2,
        scratch_shapes=[
            pltpu.VMEM(slab.shape, BF),
            pltpu.VMEM(basis.shape, BF),
            pltpu.VMEM((2, STACK, STACK), F32),
            pltpu.VMEM((2, 8 * PAGES, STACK), BF),
            pltpu.VMEM((2, STACK, 128), BF),
            pltpu.VMEM((PIECE, PIECE), BF),
            pltpu.VMEM((NV * PART, STACK), BF),
            pltpu.VMEM((NV, ROWS, CB), BF),
            pltpu.VMEM((NV, ROWS, CB), BF),
            pltpu.VMEM((32, 128), BF),
            pltpu.VMEM((NV, 32, 128), BF),
            pltpu.VMEM((NG, NV * PART, CB), BF),
            pltpu.VMEM((NV, NG, PART, CB), BF),
            pltpu.VMEM((NL, NG, PART, CB), BF),
            pltpu.VMEM((2, PAGES, 8, 128), F32),
            pltpu.VMEM((2, PAGES, 8, 128), F32),
            pltpu.VMEM((2, 8, 128), F32),
            pltpu.VMEM((2, texels, 8, 128), F32),
            pltpu.VMEM((2, 8, 128), F32),
            pltpu.VMEM((2, 4, 8, 128), F32),
            dma((NG + 1,)), dma((NV,)), dma((NV,)), dma((NG, NV)), dma((NG, NV)), dma((NV,)), dma((NV,)),
            dma((NG, NV)), dma((NG, NL)), dma((PAGES,)), dma((2, PAGES)), dma((2, texels)), dma((2, texels)),
            dma((4,)), dma((2, 4)), dma((NL,)), dma((texels,)),
        ],
        compiler_params=pltpu.CompilerParams(
            collective_id=0, has_side_effects=True, vmem_limit_bytes=40 * 1024 * 1024
        ),
    )(pltpu.with_memory_space_constraint(slab, pltpu.HBM), pltpu.with_memory_space_constraint(basis, pltpu.HBM))
    return grams[0] * view_scale, core.reshape(RB, LB, 4 * CB), grams[1] * light_scale


def solution(mesh):
    return jax.shard_map(
        body,
        mesh=mesh,
        in_specs=(P("light", "view", "texel"), P("view", None)),
        out_specs=(P("view", None), P("view", "light", "texel"), P("light", None)),
        check_vma=False,
    )
```

```python
import jax
import jax.numpy as jnp
from jax import lax
from jax.experimental import pallas as pl
from jax.experimental.pallas import tpu as pltpu
from jax.sharding import PartitionSpec as P

MESH = pl.DeviceIdType.MESH
BF = jnp.bfloat16
F32 = jnp.float32
LB = 20
VB = 20
NV = 4
NL = 4
RB = 12
CB = 256
ROWS = LB * VB
PIECE = RB * LB
NG = 5
GROUP = 4 * VB
STACK = NV * GROUP
AHEAD = 3
PART = 4 * RB
PAGES = NL * NV


def cells(shape):
    return lax.broadcasted_iota(jnp.int32, shape, 0), lax.broadcasted_iota(jnp.int32, shape, 1)


def div20(x):
    return (x * 3277) >> 16


def ones_where(condition, dtype=BF):
    return jnp.where(condition, 1.0, 0.0).astype(dtype)


def expand_table():
    row, col = cells((NV * 32, STACK))
    line = div20(col)
    return ones_where(row == 32 * (line >> 2) + col - VB * line)


def spread_table():
    row, col = cells((NV * PART, 128))
    return ones_where((row >> 2) == col)


def light_mask():
    row, col = cells((NV * PART, STACK))
    return ones_where((row & 3) == (div20(col) & 3))


def order_table():
    row, col = cells((PIECE, PIECE))
    group = (col * 1366) >> 16
    rest = col - PART * group
    return ones_where(row == LB * (rest >> 2) + 4 * group + (rest & 3))


def gram_place(g, x):
    if g:
        return 4 * (x >> 4) + (x & 3), (x >> 2) & 3
    line = div20(x)
    return 20 * (line >> 2) + x - 20 * line, line & 3


def keep_table(g):
    row, col = cells((STACK, STACK))
    return ones_where(gram_place(g, row)[1] == gram_place(g, col)[1], F32)


def pick_table(g):
    row, col = cells((8 * PAGES, STACK))
    p, q = row >> 3, row & 7
    return ones_where((q < 5) & (5 * p + q == gram_place(g, col)[0]))


def gather_table(g):
    row, col = cells((STACK, 128))
    return ones_where(gram_place(g, row)[0] == col)


def packed_tables():
    row, col = cells((3 * 64, STACK))
    piece, p, q = row >> 6, (row >> 3) & 7, row & 7
    wanted = 10 * p + jnp.where(piece == 0, q, 8 + (q >> 1))
    here = (piece == 0) | ((q < 4) & ((q & 1) == piece - 1))
    pick = ones_where(here & (wanted == gram_place(1, col)[0]))
    row, col = cells((3 * STACK, 128))
    piece = jnp.where(row >= STACK, 1, 0) + jnp.where(row >= 2 * STACK, 1, 0)
    column = gram_place(1, row - STACK * piece)[0]
    place = jnp.where(piece == 0, column, column + 120 - 40 * piece)
    low = 40 * jnp.maximum(piece - 1, 0)
    fits = (piece == 0) | ((column >= low) & (column < low + 40))
    return pick, ones_where(fits & (place == col))


def odd_share(k, t):
    return lax.rem(lax.div(k + 1 - t, 2), 2)


def share_of(k, j):
    e, t = lax.div(j, 2), lax.rem(j, 2)
    return 2 * t + lax.rem(odd_share(k, t) + 1 - e, 2)


def member_for(k, b):
    t, u = lax.div(b, 2), lax.rem(b, 2)
    return 2 * lax.rem(odd_share(k, t) + 1 + u, 2) + t


def center_of(b, n):
    t, u = lax.div(b, 2), lax.rem(b, 2)
    z = lax.rem(1 + 4 * u + 2 * t + lax.div(n, 2), 8)
    return lax.div(z, 2), 2 * lax.rem(z, 2) + lax.rem(n, 2)


def split_dot(a, b):
    def parts(x):
        hi = x.astype(BF)
        return hi, (x - hi.astype(F32)).astype(BF)

    if a.dtype == BF:
        return sum(jnp.dot(a, p, preferred_element_type=F32) for p in parts(b))
    return sum(jnp.dot(p, b, preferred_element_type=F32) for p in parts(a))


def remote(src, dst, send, recv, device):
    return pltpu.make_async_remote_copy(
        src_ref=src, dst_ref=dst, send_sem=send, recv_sem=recv, device_id=device, device_id_type=MESH
    )


def kernel(
    slab_hbm, basis_hbm,
    gram_ref, core_ref,
    slab_ref, basis_ref, keep_ref, pick_ref, gather_ref, packed_pick_ref, packed_gather_ref, order_ref, weights,
    dense, share, own_basis, all_basis, pieces, core_land, light_land,
    pages, light_pages, z_land, part, t_land, whole, last_land,
    load, basis_send, basis_recv, slab_send, slab_recv, core_send, core_recv,
    light_send, light_recv, z_send, z_recv, t_send, t_recv, last_send, last_recv, vz_send, vlast_send,
):
    texels = lax.axis_size("texel")
    tex, i, j = lax.axis_index("texel"), lax.axis_index("light"), lax.axis_index("view")
    me = i * NV + j
    mine = share_of(i, j)

    load_basis = pltpu.make_async_copy(basis_hbm, basis_ref, load.at[NG])
    load_basis.start()
    load_slab = [
        pltpu.make_async_copy(slab_hbm.at[4 * g : 4 * g + 4], slab_ref.at[4 * g : 4 * g + 4], load.at[g])
        for g in range(NG)
    ]
    for copy in load_slab:
        copy.start()
    barrier = pltpu.get_barrier_semaphore()

    def greet_z(o, c):
        other = lax.rem(me + o, PAGES)
        pl.semaphore_signal(
            barrier, inc=1, device_id=(tex, lax.div(other, NV), lax.rem(other, NV)), device_id_type=MESH
        )
        return c

    def greet_t(o, c):
        pl.semaphore_signal(barrier, inc=1, device_id=(lax.rem(tex + o, texels), i, j), device_id_type=MESH)
        return c

    lax.fori_loop(1, PAGES, greet_z, 0)
    lax.fori_loop(1, texels, greet_t, 0)

    own_basis[...] = jnp.zeros_like(own_basis)
    load_basis.wait()
    own_basis[0:VB, 0 : NV * RB] = basis_ref[...]

    def lay_out(g):
        load_slab[g].wait()
        for n in range(NV):
            for l in range(4 * g, 4 * g + 4):
                dense[n, l * VB : (l + 1) * VB, :] = slab_ref[l, :, n * CB : (n + 1) * CB]

    lay_out(0)
    pl.semaphore_wait(barrier, PAGES - 1 + texels - 1)

    others = [j, j + 1 - 2 * lax.rem(j, 2), lax.rem(j + 2, NV), NV - 1 - j]
    shares = [share_of(i, other) for other in others]

    def rows_of(g):
        return pl.ds(g * GROUP, GROUP)

    def part_of(p):
        return pl.ds(pl.multiple_of(p * PART, 16), PART)

    def slab_copy(g, o, slot):
        return remote(
            dense.at[shares[o], rows_of(g), :], share.at[slot, rows_of(g), :], slab_send.at[g, o],
            slab_recv.at[g, slot], (tex, i, others[o]),
        )

    def basis_copy(o, slot):
        return remote(own_basis, all_basis.at[slot], basis_send.at[o], basis_recv.at[slot], (tex, i, others[o]))

    for o in (2, 3, 1):
        basis_copy(o, j).start()
    local = [
        pltpu.make_async_copy(dense.at[mine, rows_of(g), :], share.at[j, rows_of(g), :], slab_recv.at[g, j])
        for g in range(NG)
    ]

    def slab_start(g):
        for o in (2, 3, 1):
            slab_copy(g, o, j).start()
        local[g].start()

    for g in range(NG):
        if g:
            lay_out(g)
        if g < AHEAD:
            slab_start(g)
    all_basis[j] = own_basis[...]
    spread, expand, mask = spread_table(), expand_table(), light_mask()
    for o in (1, 2, 3):
        basis_copy(o, others[o]).wait_recv()

    table = lax.dot_general(
        all_basis[...].reshape(NV * 32, 128), expand, (((0,), (0,)), ((), ())), preferred_element_type=F32
    ).astype(BF)
    weights[...] = jnp.dot(spread, table, preferred_element_type=F32).astype(BF) * mask

    ahead = lax.rem(1 + 4 * lax.rem(mine, 2) + 2 * lax.div(mine, 2) - 2 * i - lax.div(j, 2) + 8, 8)
    far = 1 - lax.div(ahead, 4)
    turns = [2 * far, 2 * far + 1, 2 * (1 - far), 2 * (1 - far) + 1]
    centers = [center_of(mine, p) for p in turns]

    def light_copy(g, o, ci, cj):
        return remote(
            pieces.at[g, part_of(turns[o]), :], light_land.at[i, g], light_send.at[g, o], light_recv.at[g, i],
            (tex, ci, cj),
        )

    def core_copy(o, slot, place):
        return remote(
            pieces.at[:, part_of(others[o]), :], core_land.at[place], core_send.at[o], core_recv.at[slot],
            (tex, i, others[o]),
        )

    def stack_of(g):
        return jnp.concatenate([share[s, g * GROUP : (g + 1) * GROUP, :] for s in range(NV)], axis=0)

    for g in range(NG):
        local[g].wait()
        for o in (1, 2, 3):
            slab_copy(g, o, others[o]).wait_recv()
        if g + AHEAD < NG:
            slab_start(g + AHEAD)
        pieces[g] = jnp.dot(weights[...], stack_of(g), preferred_element_type=F32).astype(BF)
        for o in range(NV):
            ci, cj = centers[o]
            here = jnp.logical_and(ci == i, cj == j)

            @pl.when(here)
            def _():
                pltpu.make_async_copy(
                    pieces.at[g, part_of(turns[o]), :], light_land.at[i, g], light_recv.at[g, i]
                ).start()

            @pl.when(jnp.logical_not(here))
            def _():
                light_copy(g, o, ci, cj).start()

    def products(stacks):
        wide = jnp.concatenate(list(stacks), axis=1)
        return lax.dot_general(wide, wide, (((1,), (1,)), ((), ())), preferred_element_type=F32)

    def to_pages(total):
        rows = split_dot(pick_ref[...], total * keep_ref[0])
        return split_dot(rows, gather_ref[...]).reshape(PAGES, 8, 128)

    def to_packed(total):
        rows = split_dot(packed_pick_ref[...], total * keep_ref[1])
        return sum(
            split_dot(rows[64 * n : 64 * n + 64], packed_gather_ref[STACK * n : STACK * n + STACK, :])
            for n in range(3)
        ).reshape(8, 8, 128)

    x, y = lax.div(tex, 4), lax.rem(tex, 4)

    def texel_at(o):
        return 4 * lax.rem(x + o // 4, 4) + lax.rem(y + o % 4, 4)

    core = lax.rem(j, 2)

    def z_copy(o, slot):
        other = lax.rem(me + o, PAGES)
        ci, cj = lax.div(other, NV), lax.rem(other, NV)
        return remote(
            light_pages.at[2 * ci + lax.rem(cj, 2)], z_land.at[1, slot(other)], z_send.at[o],
            z_recv.at[1, slot(other)], (tex, ci, cj),
        )

    def t_copy(o, slot):
        other = texel_at(o)
        return remote(
            part.at[1], t_land.at[1, slot(other)], t_send.at[1, o], t_recv.at[1, slot(other)], (other, i, j)
        )

    last_copy = remote(
        whole.at[1], last_land.at[1, core], last_send.at[0], last_recv.at[1, 0], (tex, i, others[1])
    )

    takes = j == x

    def vt_copy(o, slot):
        other = texel_at(o)
        return remote(
            pages.at[other], t_land.at[0, slot(other)], t_send.at[0, o], t_recv.at[0, slot(other)], (other, i, j)
        )

    def vz_copy(o, slot):
        return remote(
            part.at[0], z_land.at[0, slot], vz_send.at[o], z_recv.at[0, slot], (tex, lax.rem(i + o, NL), x)
        )

    def vlast_copy(o, slot):
        return remote(
            whole.at[0], last_land.at[0, slot], vlast_send.at[o], last_recv.at[0, slot], (texel_at(o), i, j)
        )

    def start_all(copy, order, own):
        for o in order:
            copy(o, lambda other: own).start()

    def wait_all(copy, order):
        for o in order:
            copy(o, lambda other: other).wait_recv()

    def sent_all(copy, order, own):
        for o in order:
            copy(o, lambda other: own).wait_send()

    z_order = (8, 7, 9, 6, 10, 5, 11, 4, 12, 3, 13, 2, 14, 1, 15)
    t_order = (10, 9, 11, 6, 14, 8, 2, 5, 7, 13, 15, 4, 12, 1, 3)

    for g in range(2):
        keep_ref[g] = keep_table(g)
    pick_ref[...] = pick_table(0)
    gather_ref[...] = gather_table(0)
    packed_pick_ref[...], packed_gather_ref[...] = packed_tables()
    pages[...] = to_pages(products(stack_of(g) for g in range(NG)))
    start_all(vt_copy, t_order, tex)
    t_land[0, tex] = pages[tex]

    for o in (2, 3, 1):
        core_copy(o, j, mine).start()
    own_piece = pltpu.make_async_copy(pieces.at[:, part_of(j), :], core_land.at[mine], core_recv.at[j])
    own_piece.start()
    order_ref[...] = order_table()

    for g in range(NG):
        for k in range(NL):
            pltpu.make_async_copy(pieces.at[g, part_of(0), :], light_land.at[k, g], light_recv.at[g, k]).wait()
    light_pages[...] = to_packed(products(
        jnp.concatenate(
            [light_land[k, g, 16 * m : 16 * m + 16, :] for k in range(NL) for g in range(NG)], axis=0
        )
        for m in range(PART // 16)
    ))
    start_all(z_copy, z_order, me)
    z_land[1, me] = light_pages[2 * i + core]

    wait_all(vt_copy, t_order)
    part[0] = jnp.sum(t_land[0], axis=0)
    for o in (2, 1, 3):
        vz_copy(o, me).start()

    @pl.when(takes)
    def _():
        z_land[0, me] = part[0]

    @pl.when(jnp.logical_not(takes))
    def _():
        vz_copy(0, me).start()

    for o in (1, 2, 3):
        basis_copy(o, j).wait_send()
        for g in range(NG):
            slab_copy(g, o, j).wait_send()
    for o in range(NV):
        ci, cj = centers[o]

        @pl.when(jnp.logical_not(jnp.logical_and(ci == i, cj == j)))
        def _():
            for g in range(NG):
                light_copy(g, o, ci, cj).wait_send()

    sent_all(vt_copy, t_order, tex)
    wait_all(z_copy, z_order)
    part[1] = jnp.sum(z_land[1], axis=0)
    start_all(t_copy, t_order, tex)
    t_land[1, tex] = part[1]

    @pl.when(takes)
    def _():
        for o in z_order:
            vz_copy(0, lax.rem(me + o, PAGES)).wait_recv()
        whole[0] = jnp.sum(z_land[0], axis=0)
        for o in t_order:
            vlast_copy(o, y).start()
        last_land[0, y] = whole[0]

    own_piece.wait()
    for o in (1, 2, 3):
        core_copy(o, others[o], shares[o]).wait_recv()
    for n in range(NV):
        core_ref[:, n * CB : (n + 1) * CB] = jnp.dot(
            order_ref[...], core_land[n].reshape(PIECE, CB), preferred_element_type=F32
        ).astype(BF)
    for o in (1, 2, 3):
        core_copy(o, j, mine).wait_send()
        vz_copy(o, me).wait_send()

    @pl.when(jnp.logical_not(takes))
    def _():
        vz_copy(0, me).wait_send()

    sent_all(z_copy, z_order, me)
    wait_all(t_copy, t_order)
    whole[1] = jnp.sum(t_land[1], axis=0)
    last_copy.start()
    last_land[1, core] = whole[1]

    for q in range(4):
        @pl.when(jnp.logical_not(jnp.logical_and(takes, y == q)))
        def _():
            vlast_copy(1, q).wait_recv()

    @pl.when(takes)
    def _():
        for o in t_order:
            vlast_copy(o, y).wait_send()

    sent_all(t_copy, t_order, tex)
    for q in range(4):
        gram_ref[0, 5 * q : 5 * q + 5, :] = last_land[0, q, 0:5, 0:80]
    last_copy.wait()
    for c in range(2):
        gram_ref[1, 10 * c : 10 * c + 8, :] = last_land[1, c, :, 0:80]
        for q in range(4):
            at = 10 * c + 8 + q // 2
            gram_ref[1, at : at + 1, 40 * (q % 2) : 40 * (q % 2) + 40] = last_land[1, c, q : q + 1, 80:120]


def body(slab, basis):
    texels = lax.axis_size("texel")
    columns_all = slab.shape[2] * texels
    view_scale = 1.0 / (LB * NL * columns_all)
    light_scale = 1.0 / (RB * NV * columns_all)
    hbm = pl.BlockSpec(memory_space=pltpu.HBM)
    vmem = pl.BlockSpec(memory_space=pltpu.VMEM)
    dma = pltpu.SemaphoreType.DMA
    grams, core = pl.pallas_call(
        kernel,
        out_shape=(
            pltpu.VMEM((2, VB, 80), F32),
            pltpu.VMEM((PIECE, 4 * CB), BF),
        ),
        in_specs=[hbm] * 2,
        out_specs=(vmem,) * 2,
        scratch_shapes=[
            pltpu.VMEM(slab.shape, BF),
            pltpu.VMEM(basis.shape, BF),
            pltpu.VMEM((2, STACK, STACK), F32),
            pltpu.VMEM((8 * PAGES, STACK), BF),
            pltpu.VMEM((STACK, 128), BF),
            pltpu.VMEM((3 * 64, STACK), BF),
            pltpu.VMEM((3 * STACK, 128), BF),
            pltpu.VMEM((PIECE, PIECE), BF),
            pltpu.VMEM((NV * PART, STACK), BF),
            pltpu.VMEM((NV, ROWS, CB), BF),
            pltpu.VMEM((NV, ROWS, CB), BF),
            pltpu.VMEM((32, 128), BF),
            pltpu.VMEM((NV, 32, 128), BF),
            pltpu.VMEM((NG, NV * PART, CB), BF),
            pltpu.VMEM((NV, NG, PART, CB), BF),
            pltpu.VMEM((NL, NG, PART, CB), BF),
            pltpu.VMEM((PAGES, 8, 128), F32),
            pltpu.VMEM((8, 8, 128), F32),
            pltpu.VMEM((2, PAGES, 8, 128), F32),
            pltpu.VMEM((2, 8, 128), F32),
            pltpu.VMEM((2, texels, 8, 128), F32),
            pltpu.VMEM((2, 8, 128), F32),
            pltpu.VMEM((2, 4, 8, 128), F32),
            dma((NG + 1,)), dma((NV,)), dma((NV,)), dma((NG, NV)), dma((NG, NV)), dma((NV,)), dma((NV,)),
            dma((NG, NV)), dma((NG, NL)), dma((PAGES,)), dma((2, PAGES)), dma((2, texels)), dma((2, texels)),
            dma((4,)), dma((2, 4)), dma((NL,)), dma((texels,)),
        ],
        compiler_params=pltpu.CompilerParams(
            collective_id=0, has_side_effects=True, vmem_limit_bytes=40 * 1024 * 1024
        ),
    )(pltpu.with_memory_space_constraint(slab, pltpu.HBM), pltpu.with_memory_space_constraint(basis, pltpu.HBM))
    return grams[0] * view_scale, core.reshape(RB, LB, 4 * CB), grams[1] * light_scale


def solution(mesh):
    return jax.shard_map(
        body,
        mesh=mesh,
        in_specs=(P("light", "view", "texel"), P("view", None)),
        out_specs=(P("view", None), P("view", "light", "texel"), P("light", None)),
        check_vma=False,
    )
```

```python
import jax
import jax.numpy as jnp
from jax import lax
from jax.experimental import pallas as pl
from jax.experimental.pallas import tpu as pltpu
from jax.sharding import PartitionSpec as P

MESH = pl.DeviceIdType.MESH
BF = jnp.bfloat16
F32 = jnp.float32
LB = 20
VB = 20
NV = 4
NL = 4
RB = 12
CB = 256
ROWS = LB * VB
PIECE = RB * LB
NG = 5
GROUP = 4 * VB
STACK = NV * GROUP
AHEAD = 3
PART = 4 * RB
PAGES = NL * NV


def cells(shape):
    return lax.broadcasted_iota(jnp.int32, shape, 0), lax.broadcasted_iota(jnp.int32, shape, 1)


def div20(x):
    return (x * 3277) >> 16


def ones_where(condition, dtype=BF):
    return jnp.where(condition, 1.0, 0.0).astype(dtype)


def expand_table():
    row, col = cells((NV * 32, STACK))
    line = div20(col)
    return ones_where(row == 32 * (line >> 2) + col - VB * line)


def spread_table():
    row, col = cells((NV * PART, 128))
    return ones_where((row >> 2) == col)


def light_mask():
    row, col = cells((NV * PART, STACK))
    return ones_where((row & 3) == (div20(col) & 3))


def order_table():
    row, col = cells((PIECE, PIECE))
    group = (col * 1366) >> 16
    rest = col - PART * group
    return ones_where(row == LB * (rest >> 2) + 4 * group + (rest & 3))


def gram_place(g, x):
    if g:
        return 4 * (x >> 4) + (x & 3), (x >> 2) & 3
    line = div20(x)
    return 20 * (line >> 2) + x - 20 * line, line & 3


def keep_table(g):
    row, col = cells((STACK, STACK))
    return ones_where(gram_place(g, row)[1] == gram_place(g, col)[1], F32)


def pick_table(g):
    row, col = cells((8 * PAGES, STACK))
    p, q = row >> 3, row & 7
    return ones_where((q < 5) & (5 * p + q == gram_place(g, col)[0]))


def gather_table(g):
    row, col = cells((STACK, 128))
    return ones_where(gram_place(g, row)[0] == col)


def packed_tables():
    row, col = cells((3 * 64, STACK))
    piece, p, q = row >> 6, (row >> 3) & 7, row & 7
    wanted = 10 * p + jnp.where(piece == 0, q, 8 + (q >> 1))
    here = (piece == 0) | ((q < 4) & ((q & 1) == piece - 1))
    pick = ones_where(here & (wanted == gram_place(1, col)[0]))
    row, col = cells((3 * STACK, 128))
    piece = jnp.where(row >= STACK, 1, 0) + jnp.where(row >= 2 * STACK, 1, 0)
    column = gram_place(1, row - STACK * piece)[0]
    place = jnp.where(piece == 0, column, column + 120 - 40 * piece)
    low = 40 * jnp.maximum(piece - 1, 0)
    fits = (piece == 0) | ((column >= low) & (column < low + 40))
    return pick, ones_where(fits & (place == col))


def odd_share(k, t):
    return lax.rem(lax.div(k + 1 - t, 2), 2)


def share_of(k, j):
    e, t = lax.div(j, 2), lax.rem(j, 2)
    return 2 * t + lax.rem(odd_share(k, t) + 1 - e, 2)


def member_for(k, b):
    t, u = lax.div(b, 2), lax.rem(b, 2)
    return 2 * lax.rem(odd_share(k, t) + 1 + u, 2) + t


def center_of(b, n):
    t, u = lax.div(b, 2), lax.rem(b, 2)
    z = lax.rem(1 + 4 * u + 2 * t + lax.div(n, 2), 8)
    return lax.div(z, 2), 2 * lax.rem(z, 2) + lax.rem(n, 2)


def split_dot(a, b):
    def parts(x):
        hi = x.astype(BF)
        return hi, (x - hi.astype(F32)).astype(BF)

    if a.dtype == BF:
        return sum(jnp.dot(a, p, preferred_element_type=F32) for p in parts(b))
    return sum(jnp.dot(p, b, preferred_element_type=F32) for p in parts(a))


def remote(src, dst, send, recv, device):
    return pltpu.make_async_remote_copy(
        src_ref=src, dst_ref=dst, send_sem=send, recv_sem=recv, device_id=device, device_id_type=MESH
    )


def kernel(
    slab_hbm, basis_hbm,
    gram_ref, core_ref,
    slab_ref, basis_ref, keep_ref, pick_ref, gather_ref, packed_pick_ref, packed_gather_ref, order_ref, weights,
    dense, share, own_basis, all_basis, pieces, core_land, light_land,
    pages, light_pages, z_land, part, t_land, whole, last_land,
    load, basis_send, basis_recv, slab_send, slab_recv, core_send, core_recv,
    light_send, light_recv, z_send, z_recv, t_send, t_recv, last_send, last_recv, vz_send, vlast_send,
):
    texels = lax.axis_size("texel")
    tex, i, j = lax.axis_index("texel"), lax.axis_index("light"), lax.axis_index("view")
    me = i * NV + j
    mine = share_of(i, j)

    load_basis = pltpu.make_async_copy(basis_hbm, basis_ref, load.at[NG])
    load_basis.start()
    load_slab = [
        pltpu.make_async_copy(slab_hbm.at[4 * g : 4 * g + 4], slab_ref.at[4 * g : 4 * g + 4], load.at[g])
        for g in range(NG)
    ]
    for copy in load_slab:
        copy.start()
    barrier = pltpu.get_barrier_semaphore()

    def greet_z(o, c):
        other = lax.rem(me + o, PAGES)
        pl.semaphore_signal(
            barrier, inc=1, device_id=(tex, lax.div(other, NV), lax.rem(other, NV)), device_id_type=MESH
        )
        return c

    def greet_t(o, c):
        pl.semaphore_signal(barrier, inc=1, device_id=(lax.rem(tex + o, texels), i, j), device_id_type=MESH)
        return c

    lax.fori_loop(1, PAGES, greet_z, 0)
    lax.fori_loop(1, texels, greet_t, 0)

    own_basis[...] = jnp.zeros_like(own_basis)
    load_basis.wait()
    own_basis[0:VB, 0 : NV * RB] = basis_ref[...]

    def lay_out(g):
        load_slab[g].wait()
        for n in range(NV):
            for l in range(4 * g, 4 * g + 4):
                dense[n, l * VB : (l + 1) * VB, :] = slab_ref[l, :, n * CB : (n + 1) * CB]

    lay_out(0)
    pl.semaphore_wait(barrier, PAGES - 1 + texels - 1)

    others = [j, j + 1 - 2 * lax.rem(j, 2), lax.rem(j + 2, NV), NV - 1 - j]
    shares = [share_of(i, other) for other in others]

    def rows_of(g):
        return pl.ds(g * GROUP, GROUP)

    def part_of(p):
        return pl.ds(pl.multiple_of(p * PART, 16), PART)

    def slab_copy(g, o, slot):
        return remote(
            dense.at[shares[o], rows_of(g), :], share.at[slot, rows_of(g), :], slab_send.at[g, o],
            slab_recv.at[g, slot], (tex, i, others[o]),
        )

    def basis_copy(o, slot):
        return remote(own_basis, all_basis.at[slot], basis_send.at[o], basis_recv.at[slot], (tex, i, others[o]))

    for o in (2, 3, 1):
        basis_copy(o, j).start()
    local = [
        pltpu.make_async_copy(dense.at[mine, rows_of(g), :], share.at[j, rows_of(g), :], slab_recv.at[g, j])
        for g in range(NG)
    ]

    def slab_start(g):
        for o in (2, 3, 1):
            slab_copy(g, o, j).start()
        local[g].start()

    for g in range(NG):
        if g:
            lay_out(g)
        if g < AHEAD:
            slab_start(g)
    all_basis[j] = own_basis[...]
    spread, expand, mask = spread_table(), expand_table(), light_mask()
    for o in (1, 2, 3):
        basis_copy(o, others[o]).wait_recv()

    table = lax.dot_general(
        all_basis[...].reshape(NV * 32, 128), expand, (((0,), (0,)), ((), ())), preferred_element_type=F32
    ).astype(BF)
    weights[...] = jnp.dot(spread, table, preferred_element_type=F32).astype(BF) * mask

    ahead = lax.rem(1 + 4 * lax.rem(mine, 2) + 2 * lax.div(mine, 2) - 2 * i - lax.div(j, 2) + 8, 8)
    far = 1 - lax.div(ahead, 4)
    turns = [2 * far, 2 * far + 1, 2 * (1 - far), 2 * (1 - far) + 1]
    centers = [center_of(mine, p) for p in turns]

    def light_copy(g, o, ci, cj):
        return remote(
            pieces.at[g, part_of(turns[o]), :], light_land.at[i, g], light_send.at[g, o], light_recv.at[g, i],
            (tex, ci, cj),
        )

    def core_copy(o, slot, place):
        return remote(
            pieces.at[:, part_of(others[o]), :], core_land.at[place], core_send.at[o], core_recv.at[slot],
            (tex, i, others[o]),
        )

    def stack_of(g):
        return jnp.concatenate([share[s, g * GROUP : (g + 1) * GROUP, :] for s in range(NV)], axis=0)

    for g in range(NG):
        local[g].wait()
        for o in (1, 2, 3):
            slab_copy(g, o, others[o]).wait_recv()
        if g + AHEAD < NG:
            slab_start(g + AHEAD)
        pieces[g] = jnp.dot(weights[...], stack_of(g), preferred_element_type=F32).astype(BF)
        for o in range(NV):
            ci, cj = centers[o]
            here = jnp.logical_and(ci == i, cj == j)

            @pl.when(here)
            def _():
                pltpu.make_async_copy(
                    pieces.at[g, part_of(turns[o]), :], light_land.at[i, g], light_recv.at[g, i]
                ).start()

            @pl.when(jnp.logical_not(here))
            def _():
                light_copy(g, o, ci, cj).start()

    def products(stacks):
        wide = jnp.concatenate(list(stacks), axis=1)
        return lax.dot_general(wide, wide, (((1,), (1,)), ((), ())), preferred_element_type=F32)

    def to_pages(total):
        rows = split_dot(pick_ref[...], total * keep_ref[0])
        return split_dot(rows, gather_ref[...]).reshape(PAGES, 8, 128)

    def to_packed(total):
        rows = split_dot(packed_pick_ref[...], total * keep_ref[1])
        return sum(
            split_dot(rows[64 * n : 64 * n + 64], packed_gather_ref[STACK * n : STACK * n + STACK, :])
            for n in range(3)
        ).reshape(8, 8, 128)

    x, y = lax.div(tex, 4), lax.rem(tex, 4)

    def texel_at(o):
        return 4 * lax.rem(x + o // 4, 4) + lax.rem(y + o % 4, 4)

    sums = jnp.logical_or(j == 0, j == 3)
    core = lax.div(j, 2)

    def z_copy(d, c):
        ci = lax.rem(i + d, NL)
        return remote(
            light_pages.at[2 * ci + c], z_land.at[1, me], z_send.at[2 * d + c], z_recv.at[1, me], (tex, ci, 3 * c)
        )

    def z_landed(o):
        source = lax.rem(me + o, PAGES)
        return remote(
            light_pages.at[0], z_land.at[1, source], z_send.at[0], z_recv.at[1, source], (tex, i, others[1])
        )

    def t_copy(o, slot):
        other = texel_at(o)
        return remote(
            part.at[1], t_land.at[1, slot(other)], t_send.at[1, o], t_recv.at[1, slot(other)], (other, i, j)
        )

    def last_copy(o):
        return remote(
            whole.at[1], last_land.at[1, core], last_send.at[o], last_recv.at[1, core], (tex, i, others[o])
        )

    def last_landed(c):
        return remote(
            whole.at[1], last_land.at[1, c], last_send.at[1], last_recv.at[1, c], (tex, i, others[1])
        )

    takes = j == x

    def vt_copy(o, slot):
        other = texel_at(o)
        return remote(
            pages.at[other], t_land.at[0, slot(other)], t_send.at[0, o], t_recv.at[0, slot(other)], (other, i, j)
        )

    def vz_copy(o, slot):
        return remote(
            part.at[0], z_land.at[0, slot], vz_send.at[o], z_recv.at[0, slot], (tex, lax.rem(i + o, NL), x)
        )

    def vlast_copy(o, slot):
        return remote(
            whole.at[0], last_land.at[0, slot], vlast_send.at[o], last_recv.at[0, slot], (texel_at(o), i, j)
        )

    def start_all(copy, order, own):
        for o in order:
            copy(o, lambda other: own).start()

    def wait_all(copy, order):
        for o in order:
            copy(o, lambda other: other).wait_recv()

    def sent_all(copy, order, own):
        for o in order:
            copy(o, lambda other: own).wait_send()

    z_order = (8, 7, 9, 6, 10, 5, 11, 4, 12, 3, 13, 2, 14, 1, 15)
    t_order = (10, 9, 11, 6, 14, 8, 2, 5, 7, 13, 15, 4, 12, 1, 3)

    for g in range(2):
        keep_ref[g] = keep_table(g)
    pick_ref[...] = pick_table(0)
    gather_ref[...] = gather_table(0)
    packed_pick_ref[...], packed_gather_ref[...] = packed_tables()
    pages[...] = to_pages(products(stack_of(g) for g in range(NG)))
    start_all(vt_copy, t_order, tex)
    t_land[0, tex] = pages[tex]

    for o in (2, 3, 1):
        core_copy(o, j, mine).start()
    own_piece = pltpu.make_async_copy(pieces.at[:, part_of(j), :], core_land.at[mine], core_recv.at[j])
    own_piece.start()
    order_ref[...] = order_table()

    for g in range(NG):
        for k in range(NL):
            pltpu.make_async_copy(pieces.at[g, part_of(0), :], light_land.at[k, g], light_recv.at[g, k]).wait()
    light_pages[...] = to_packed(products(
        jnp.concatenate(
            [light_land[k, g, 16 * m : 16 * m + 16, :] for k in range(NL) for g in range(NG)], axis=0
        )
        for m in range(PART // 16)
    ))
    for d in (2, 1, 3):
        for c in range(2):
            z_copy(d, c).start()
    for c in range(2):
        @pl.when(j == 3 * c)
        def _():
            z_land[1, me] = light_pages[2 * i + c]

        @pl.when(j != 3 * c)
        def _():
            z_copy(0, c).start()


    wait_all(vt_copy, t_order)
    part[0] = jnp.sum(t_land[0], axis=0)
    for o in (2, 1, 3):
        vz_copy(o, me).start()

    @pl.when(takes)
    def _():
        z_land[0, me] = part[0]

    @pl.when(jnp.logical_not(takes))
    def _():
        vz_copy(0, me).start()

    for o in (1, 2, 3):
        basis_copy(o, j).wait_send()
        for g in range(NG):
            slab_copy(g, o, j).wait_send()
    for o in range(NV):
        ci, cj = centers[o]

        @pl.when(jnp.logical_not(jnp.logical_and(ci == i, cj == j)))
        def _():
            for g in range(NG):
                light_copy(g, o, ci, cj).wait_send()

    sent_all(vt_copy, t_order, tex)
    @pl.when(takes)
    def _():
        for o in z_order:
            vz_copy(0, lax.rem(me + o, PAGES)).wait_recv()
        whole[0] = jnp.sum(z_land[0], axis=0)
        for o in t_order:
            vlast_copy(o, y).start()
        last_land[0, y] = whole[0]

    @pl.when(sums)
    def _():
        for o in z_order:
            z_landed(o).wait_recv()
        part[1] = jnp.sum(z_land[1], axis=0)
        start_all(t_copy, t_order, tex)
        t_land[1, tex] = part[1]

    own_piece.wait()
    for o in (1, 2, 3):
        core_copy(o, others[o], shares[o]).wait_recv()
    for n in range(NV):
        core_ref[:, n * CB : (n + 1) * CB] = jnp.dot(
            order_ref[...], core_land[n].reshape(PIECE, CB), preferred_element_type=F32
        ).astype(BF)
    for o in (1, 2, 3):
        core_copy(o, j, mine).wait_send()
        vz_copy(o, me).wait_send()

    @pl.when(jnp.logical_not(takes))
    def _():
        vz_copy(0, me).wait_send()

    for d in (2, 1, 3):
        for c in range(2):
            z_copy(d, c).wait_send()
    for c in range(2):
        @pl.when(j != 3 * c)
        def _():
            z_copy(0, c).wait_send()

    @pl.when(sums)
    def _():
        wait_all(t_copy, t_order)
        whole[1] = jnp.sum(t_land[1], axis=0)
        for o in (2, 3, 1):
            last_copy(o).start()
        last_land[1, core] = whole[1]

    for q in range(4):
        @pl.when(jnp.logical_not(jnp.logical_and(takes, y == q)))
        def _():
            vlast_copy(1, q).wait_recv()

    @pl.when(takes)
    def _():
        for o in t_order:
            vlast_copy(o, y).wait_send()

    @pl.when(sums)
    def _():
        sent_all(t_copy, t_order, tex)

    for q in range(4):
        gram_ref[0, 5 * q : 5 * q + 5, :] = last_land[0, q, 0:5, 0:80]
    for c in range(2):
        @pl.when(j != 3 * c)
        def _():
            last_landed(c).wait_recv()

    @pl.when(sums)
    def _():
        for o in (2, 3, 1):
            last_copy(o).wait_send()

    for c in range(2):
        gram_ref[1, 10 * c : 10 * c + 8, :] = last_land[1, c, :, 0:80]
        for q in range(4):
            at = 10 * c + 8 + q // 2
            gram_ref[1, at : at + 1, 40 * (q % 2) : 40 * (q % 2) + 40] = last_land[1, c, q : q + 1, 80:120]


def body(slab, basis):
    texels = lax.axis_size("texel")
    columns_all = slab.shape[2] * texels
    view_scale = 1.0 / (LB * NL * columns_all)
    light_scale = 1.0 / (RB * NV * columns_all)
    hbm = pl.BlockSpec(memory_space=pltpu.HBM)
    vmem = pl.BlockSpec(memory_space=pltpu.VMEM)
    dma = pltpu.SemaphoreType.DMA
    grams, core = pl.pallas_call(
        kernel,
        out_shape=(
            pltpu.VMEM((2, VB, 80), F32),
            pltpu.VMEM((PIECE, 4 * CB), BF),
        ),
        in_specs=[hbm] * 2,
        out_specs=(vmem,) * 2,
        scratch_shapes=[
            pltpu.VMEM(slab.shape, BF),
            pltpu.VMEM(basis.shape, BF),
            pltpu.VMEM((2, STACK, STACK), F32),
            pltpu.VMEM((8 * PAGES, STACK), BF),
            pltpu.VMEM((STACK, 128), BF),
            pltpu.VMEM((3 * 64, STACK), BF),
            pltpu.VMEM((3 * STACK, 128), BF),
            pltpu.VMEM((PIECE, PIECE), BF),
            pltpu.VMEM((NV * PART, STACK), BF),
            pltpu.VMEM((NV, ROWS, CB), BF),
            pltpu.VMEM((NV, ROWS, CB), BF),
            pltpu.VMEM((32, 128), BF),
            pltpu.VMEM((NV, 32, 128), BF),
            pltpu.VMEM((NG, NV * PART, CB), BF),
            pltpu.VMEM((NV, NG, PART, CB), BF),
            pltpu.VMEM((NL, NG, PART, CB), BF),
            pltpu.VMEM((PAGES, 8, 128), F32),
            pltpu.VMEM((8, 8, 128), F32),
            pltpu.VMEM((2, PAGES, 8, 128), F32),
            pltpu.VMEM((2, 8, 128), F32),
            pltpu.VMEM((2, texels, 8, 128), F32),
            pltpu.VMEM((2, 8, 128), F32),
            pltpu.VMEM((2, 4, 8, 128), F32),
            dma((NG + 1,)), dma((NV,)), dma((NV,)), dma((NG, NV)), dma((NG, NV)), dma((NV,)), dma((NV,)),
            dma((NG, NV)), dma((NG, NL)), dma((PAGES,)), dma((2, PAGES)), dma((2, texels)), dma((2, texels)),
            dma((4,)), dma((2, 4)), dma((NL,)), dma((texels,)),
        ],
        compiler_params=pltpu.CompilerParams(
            collective_id=0, has_side_effects=True, vmem_limit_bytes=40 * 1024 * 1024
        ),
    )(pltpu.with_memory_space_constraint(slab, pltpu.HBM), pltpu.with_memory_space_constraint(basis, pltpu.HBM))
    return grams[0] * view_scale, core.reshape(RB, LB, 4 * CB), grams[1] * light_scale


def solution(mesh):
    return jax.shard_map(
        body,
        mesh=mesh,
        in_specs=(P("light", "view", "texel"), P("view", None)),
        out_specs=(P("view", None), P("view", "light", "texel"), P("light", None)),
        check_vma=False,
    )
```

```python
import jax
import jax.numpy as jnp
from jax import lax
from jax.experimental import pallas as pl
from jax.experimental.pallas import tpu as pltpu
from jax.sharding import PartitionSpec as P

MESH = pl.DeviceIdType.MESH
BF = jnp.bfloat16
F32 = jnp.float32
LB = 20
VB = 20
NV = 4
NL = 4
RB = 12
CB = 256
ROWS = LB * VB
PIECE = RB * LB
NG = 5
GROUP = 4 * VB
STACK = NV * GROUP
AHEAD = 4
PART = 4 * RB
PAGES = NL * NV


def cells(shape):
    return lax.broadcasted_iota(jnp.int32, shape, 0), lax.broadcasted_iota(jnp.int32, shape, 1)


def div20(x):
    return (x * 3277) >> 16


def ones_where(condition, dtype=BF):
    return jnp.where(condition, 1.0, 0.0).astype(dtype)


def expand_table():
    row, col = cells((NV * 32, STACK))
    line = div20(col)
    return ones_where(row == 32 * (line >> 2) + col - VB * line)


def spread_table():
    row, col = cells((NV * PART, 128))
    return ones_where((row >> 2) == col)


def light_mask():
    row, col = cells((NV * PART, STACK))
    return ones_where((row & 3) == (div20(col) & 3))


def order_table():
    row, col = cells((PIECE, PIECE))
    group = (col * 1366) >> 16
    rest = col - PART * group
    return ones_where(row == LB * (rest >> 2) + 4 * group + (rest & 3))


def gram_place(g, x):
    if g:
        return 4 * (x >> 4) + (x & 3), (x >> 2) & 3
    line = div20(x)
    return 20 * (line >> 2) + x - 20 * line, line & 3


def keep_table(g):
    row, col = cells((STACK, STACK))
    return ones_where(gram_place(g, row)[1] == gram_place(g, col)[1], F32)


def pick_table(g):
    row, col = cells((8 * PAGES, STACK))
    p, q = row >> 3, row & 7
    return ones_where((q < 5) & (5 * p + q == gram_place(g, col)[0]))


def gather_table(g):
    row, col = cells((STACK, 128))
    return ones_where(gram_place(g, row)[0] == col)


def packed_tables():
    row, col = cells((3 * 64, STACK))
    piece, p, q = row >> 6, (row >> 3) & 7, row & 7
    wanted = 10 * p + jnp.where(piece == 0, q, 8 + (q >> 1))
    here = (piece == 0) | ((q < 4) & ((q & 1) == piece - 1))
    pick = ones_where(here & (wanted == gram_place(1, col)[0]))
    row, col = cells((3 * STACK, 128))
    piece = jnp.where(row >= STACK, 1, 0) + jnp.where(row >= 2 * STACK, 1, 0)
    column = gram_place(1, row - STACK * piece)[0]
    place = jnp.where(piece == 0, column, column + 120 - 40 * piece)
    low = 40 * jnp.maximum(piece - 1, 0)
    fits = (piece == 0) | ((column >= low) & (column < low + 40))
    return pick, ones_where(fits & (place == col))


def odd_share(k, t):
    return lax.rem(lax.div(k + 1 - t, 2), 2)


def share_of(k, j):
    e, t = lax.div(j, 2), lax.rem(j, 2)
    return 2 * t + lax.rem(odd_share(k, t) + 1 - e, 2)


def member_for(k, b):
    t, u = lax.div(b, 2), lax.rem(b, 2)
    return 2 * lax.rem(odd_share(k, t) + 1 + u, 2) + t


def center_of(b, n):
    t, u = lax.div(b, 2), lax.rem(b, 2)
    z = lax.rem(1 + 4 * u + 2 * t + lax.div(n, 2), 8)
    return lax.div(z, 2), 2 * lax.rem(z, 2) + lax.rem(n, 2)


def split_dot(a, b):
    def parts(x):
        hi = x.astype(BF)
        return hi, (x - hi.astype(F32)).astype(BF)

    if a.dtype == BF:
        return sum(jnp.dot(a, p, preferred_element_type=F32) for p in parts(b))
    return sum(jnp.dot(p, b, preferred_element_type=F32) for p in parts(a))


def remote(src, dst, send, recv, device):
    return pltpu.make_async_remote_copy(
        src_ref=src, dst_ref=dst, send_sem=send, recv_sem=recv, device_id=device, device_id_type=MESH
    )


def kernel(
    slab_hbm, basis_hbm,
    gram_ref, core_ref,
    slab_ref, basis_ref, keep_ref, pick_ref, gather_ref, packed_pick_ref, packed_gather_ref, order_ref, weights,
    dense, share, own_basis, all_basis, pieces, core_land, light_land,
    pages, light_pages, z_land, part, t_land, whole, last_land,
    load, basis_send, basis_recv, slab_send, slab_recv, core_send, core_recv,
    light_send, light_recv, z_send, z_recv, t_send, t_recv, last_send, last_recv, vz_send, vlast_send,
):
    texels = lax.axis_size("texel")
    tex, i, j = lax.axis_index("texel"), lax.axis_index("light"), lax.axis_index("view")
    me = i * NV + j
    mine = share_of(i, j)

    load_basis = pltpu.make_async_copy(basis_hbm, basis_ref, load.at[NG])
    load_basis.start()
    load_slab = [
        pltpu.make_async_copy(slab_hbm.at[4 * g : 4 * g + 4], slab_ref.at[4 * g : 4 * g + 4], load.at[g])
        for g in range(NG)
    ]
    for copy in load_slab:
        copy.start()
    barrier = pltpu.get_barrier_semaphore()

    def greet(device):
        pl.semaphore_signal(barrier, inc=1, device_id=device, device_id_type=MESH)

    for o in (1, 2, 3):
        greet((tex, i, lax.rem(j + o, NV)))
    for d in (2, 1, 3):
        for o in range(NV):
            greet((tex, lax.rem(i + d, NL), o))
    for o in range(1, texels):
        greet((lax.rem(tex + o, texels), i, j))

    own_basis[...] = jnp.zeros_like(own_basis)
    load_basis.wait()
    own_basis[0:VB, 0 : NV * RB] = basis_ref[...]

    def lay_out(g):
        load_slab[g].wait()
        for n in range(NV):
            for l in range(4 * g, 4 * g + 4):
                dense[n, l * VB : (l + 1) * VB, :] = slab_ref[l, :, n * CB : (n + 1) * CB]

    lay_out(0)
    pl.semaphore_wait(barrier, PAGES - 1 + texels - 1)

    others = [j, j + 1 - 2 * lax.rem(j, 2), lax.rem(j + 2, NV), NV - 1 - j]
    shares = [share_of(i, other) for other in others]

    def rows_of(g):
        return pl.ds(g * GROUP, GROUP)

    def part_of(p):
        return pl.ds(pl.multiple_of(p * PART, 16), PART)

    def slab_copy(g, o, slot):
        return remote(
            dense.at[shares[o], rows_of(g), :], share.at[slot, rows_of(g), :], slab_send.at[g, o],
            slab_recv.at[g, slot], (tex, i, others[o]),
        )

    def basis_copy(o, slot):
        return remote(own_basis, all_basis.at[slot], basis_send.at[o], basis_recv.at[slot], (tex, i, others[o]))

    for o in (2, 3, 1):
        basis_copy(o, j).start()
    local = [
        pltpu.make_async_copy(dense.at[mine, rows_of(g), :], share.at[j, rows_of(g), :], slab_recv.at[g, j])
        for g in range(NG)
    ]

    def slab_start(g):
        for o in (2, 3, 1):
            slab_copy(g, o, j).start()
        local[g].start()

    for g in range(NG):
        if g:
            lay_out(g)
        if g < AHEAD:
            slab_start(g)
    all_basis[j] = own_basis[...]
    spread, expand, mask = spread_table(), expand_table(), light_mask()
    for o in (1, 2, 3):
        basis_copy(o, others[o]).wait_recv()

    table = lax.dot_general(
        all_basis[...].reshape(NV * 32, 128), expand, (((0,), (0,)), ((), ())), preferred_element_type=F32
    ).astype(BF)
    weights[...] = jnp.dot(spread, table, preferred_element_type=F32).astype(BF) * mask

    ahead = lax.rem(1 + 4 * lax.rem(mine, 2) + 2 * lax.div(mine, 2) - 2 * i - lax.div(j, 2) + 8, 8)
    far = 1 - lax.div(ahead, 4)
    turns = [2 * far, 2 * far + 1, 2 * (1 - far), 2 * (1 - far) + 1]
    centers = [center_of(mine, p) for p in turns]

    def light_copy(g, o, ci, cj):
        return remote(
            pieces.at[g, part_of(turns[o]), :], light_land.at[i, g], light_send.at[g, o], light_recv.at[g, i],
            (tex, ci, cj),
        )

    def core_copy(o, slot, place):
        return remote(
            pieces.at[:, part_of(others[o]), :], core_land.at[place], core_send.at[o], core_recv.at[slot],
            (tex, i, others[o]),
        )

    def stack_of(g):
        return jnp.concatenate([share[s, g * GROUP : (g + 1) * GROUP, :] for s in range(NV)], axis=0)

    for g in range(NG):
        local[g].wait()
        for o in (1, 2, 3):
            slab_copy(g, o, others[o]).wait_recv()
        if g + AHEAD < NG:
            slab_start(g + AHEAD)
        pieces[g] = jnp.dot(weights[...], stack_of(g), preferred_element_type=F32).astype(BF)
        for o in range(NV):
            ci, cj = centers[o]
            here = jnp.logical_and(ci == i, cj == j)

            @pl.when(here)
            def _():
                pltpu.make_async_copy(
                    pieces.at[g, part_of(turns[o]), :], light_land.at[i, g], light_recv.at[g, i]
                ).start()

            @pl.when(jnp.logical_not(here))
            def _():
                light_copy(g, o, ci, cj).start()

    def products(stacks):
        wide = jnp.concatenate(list(stacks), axis=1)
        return lax.dot_general(wide, wide, (((1,), (1,)), ((), ())), preferred_element_type=F32)

    def to_pages(total):
        rows = split_dot(pick_ref[...], total * keep_ref[0])
        return split_dot(rows, gather_ref[...]).reshape(PAGES, 8, 128)

    def to_packed(total):
        rows = split_dot(packed_pick_ref[...], total * keep_ref[1])
        return sum(
            split_dot(rows[64 * n : 64 * n + 64], packed_gather_ref[STACK * n : STACK * n + STACK, :])
            for n in range(3)
        ).reshape(8, 8, 128)

    x, y = lax.div(tex, 4), lax.rem(tex, 4)

    def texel_at(o):
        return 4 * lax.rem(x + o // 4, 4) + lax.rem(y + o % 4, 4)

    sums = jnp.logical_or(j == 0, j == 3)
    core = lax.div(j, 2)

    def z_copy(d, c):
        ci = lax.rem(i + d, NL)
        return remote(
            light_pages.at[2 * ci + c], z_land.at[1, me], z_send.at[2 * d + c], z_recv.at[1, me], (tex, ci, 3 * c)
        )

    def z_landed(o):
        source = lax.rem(me + o, PAGES)
        return remote(
            light_pages.at[0], z_land.at[1, source], z_send.at[0], z_recv.at[1, source], (tex, i, others[1])
        )

    def t_copy(o, slot):
        other = texel_at(o)
        return remote(
            part.at[1], t_land.at[1, slot(other)], t_send.at[1, o], t_recv.at[1, slot(other)], (other, i, j)
        )

    def last_copy(o):
        return remote(
            whole.at[1], last_land.at[1, core], last_send.at[o], last_recv.at[1, core], (tex, i, others[o])
        )

    def last_landed(c):
        return remote(
            whole.at[1], last_land.at[1, c], last_send.at[1], last_recv.at[1, c], (tex, i, others[1])
        )

    takes = j == x

    def vt_copy(o, slot):
        other = texel_at(o)
        return remote(
            pages.at[other], t_land.at[0, slot(other)], t_send.at[0, o], t_recv.at[0, slot(other)], (other, i, j)
        )

    def vz_copy(o, slot):
        return remote(
            part.at[0], z_land.at[0, slot], vz_send.at[o], z_recv.at[0, slot], (tex, lax.rem(i + o, NL), x)
        )

    def vlast_copy(o, slot):
        return remote(
            whole.at[0], last_land.at[0, slot], vlast_send.at[o], last_recv.at[0, slot], (texel_at(o), i, j)
        )

    def start_all(copy, order, own):
        for o in order:
            copy(o, lambda other: own).start()

    def wait_all(copy, order):
        for o in order:
            copy(o, lambda other: other).wait_recv()

    def sent_all(copy, order, own):
        for o in order:
            copy(o, lambda other: own).wait_send()

    z_order = (8, 7, 9, 6, 10, 5, 11, 4, 12, 3, 13, 2, 14, 1, 15)
    t_order = (10, 9, 11, 6, 14, 8, 2, 5, 7, 13, 15, 4, 12, 1, 3)

    for g in range(2):
        keep_ref[g] = keep_table(g)
    pick_ref[...] = pick_table(0)
    gather_ref[...] = gather_table(0)
    packed_pick_ref[...], packed_gather_ref[...] = packed_tables()
    pages[...] = to_pages(products(stack_of(g) for g in range(NG)))
    start_all(vt_copy, t_order, tex)
    t_land[0, tex] = pages[tex]

    for o in (2, 3, 1):
        core_copy(o, j, mine).start()
    own_piece = pltpu.make_async_copy(pieces.at[:, part_of(j), :], core_land.at[mine], core_recv.at[j])
    own_piece.start()
    order_ref[...] = order_table()

    for g in range(NG):
        for k in range(NL):
            pltpu.make_async_copy(pieces.at[g, part_of(0), :], light_land.at[k, g], light_recv.at[g, k]).wait()
    light_pages[...] = to_packed(products(
        jnp.concatenate(
            [light_land[k, g, 16 * m : 16 * m + 16, :] for k in range(NL) for g in range(NG)], axis=0
        )
        for m in range(PART // 16)
    ))
    for d in (2, 1, 3):
        for c in range(2):
            z_copy(d, c).start()
    for c in range(2):
        @pl.when(j == 3 * c)
        def _():
            z_land[1, me] = light_pages[2 * i + c]

        @pl.when(j != 3 * c)
        def _():
            z_copy(0, c).start()


    wait_all(vt_copy, t_order)
    part[0] = jnp.sum(t_land[0], axis=0)
    for o in (2, 1, 3):
        vz_copy(o, me).start()

    @pl.when(takes)
    def _():
        z_land[0, me] = part[0]

    @pl.when(jnp.logical_not(takes))
    def _():
        vz_copy(0, me).start()

    for o in (1, 2, 3):
        basis_copy(o, j).wait_send()
        for g in range(NG):
            slab_copy(g, o, j).wait_send()
    for o in range(NV):
        ci, cj = centers[o]

        @pl.when(jnp.logical_not(jnp.logical_and(ci == i, cj == j)))
        def _():
            for g in range(NG):
                light_copy(g, o, ci, cj).wait_send()

    sent_all(vt_copy, t_order, tex)
    @pl.when(takes)
    def _():
        for o in z_order:
            vz_copy(0, lax.rem(me + o, PAGES)).wait_recv()
        whole[0] = jnp.sum(z_land[0], axis=0)
        for o in t_order:
            vlast_copy(o, y).start()
        last_land[0, y] = whole[0]

    @pl.when(sums)
    def _():
        for o in z_order:
            z_landed(o).wait_recv()
        part[1] = jnp.sum(z_land[1], axis=0)
        start_all(t_copy, t_order, tex)
        t_land[1, tex] = part[1]

    own_piece.wait()
    for o in (1, 2, 3):
        core_copy(o, others[o], shares[o]).wait_recv()
    for n in range(NV):
        core_ref[:, n * CB : (n + 1) * CB] = jnp.dot(
            order_ref[...], core_land[n].reshape(PIECE, CB), preferred_element_type=F32
        ).astype(BF)
    for o in (1, 2, 3):
        core_copy(o, j, mine).wait_send()
        vz_copy(o, me).wait_send()

    @pl.when(jnp.logical_not(takes))
    def _():
        vz_copy(0, me).wait_send()

    for d in (2, 1, 3):
        for c in range(2):
            z_copy(d, c).wait_send()
    for c in range(2):
        @pl.when(j != 3 * c)
        def _():
            z_copy(0, c).wait_send()

    @pl.when(sums)
    def _():
        wait_all(t_copy, t_order)
        whole[1] = jnp.sum(t_land[1], axis=0)
        for o in (2, 3, 1):
            last_copy(o).start()
        last_land[1, core] = whole[1]

    for q in range(4):
        @pl.when(jnp.logical_not(jnp.logical_and(takes, y == q)))
        def _():
            vlast_copy(1, q).wait_recv()

    @pl.when(takes)
    def _():
        for o in t_order:
            vlast_copy(o, y).wait_send()

    @pl.when(sums)
    def _():
        sent_all(t_copy, t_order, tex)

    for q in range(4):
        gram_ref[0, 5 * q : 5 * q + 5, :] = last_land[0, q, 0:5, 0:80]
    for c in range(2):
        @pl.when(j != 3 * c)
        def _():
            last_landed(c).wait_recv()

    @pl.when(sums)
    def _():
        for o in (2, 3, 1):
            last_copy(o).wait_send()

    for c in range(2):
        gram_ref[1, 10 * c : 10 * c + 8, :] = last_land[1, c, :, 0:80]
        for q in range(4):
            at = 10 * c + 8 + q // 2
            gram_ref[1, at : at + 1, 40 * (q % 2) : 40 * (q % 2) + 40] = last_land[1, c, q : q + 1, 80:120]


def body(slab, basis):
    texels = lax.axis_size("texel")
    columns_all = slab.shape[2] * texels
    view_scale = 1.0 / (LB * NL * columns_all)
    light_scale = 1.0 / (RB * NV * columns_all)
    hbm = pl.BlockSpec(memory_space=pltpu.HBM)
    vmem = pl.BlockSpec(memory_space=pltpu.VMEM)
    dma = pltpu.SemaphoreType.DMA
    grams, core = pl.pallas_call(
        kernel,
        out_shape=(
            pltpu.VMEM((2, VB, 80), F32),
            pltpu.VMEM((PIECE, 4 * CB), BF),
        ),
        in_specs=[hbm] * 2,
        out_specs=(vmem,) * 2,
        scratch_shapes=[
            pltpu.VMEM(slab.shape, BF),
            pltpu.VMEM(basis.shape, BF),
            pltpu.VMEM((2, STACK, STACK), F32),
            pltpu.VMEM((8 * PAGES, STACK), BF),
            pltpu.VMEM((STACK, 128), BF),
            pltpu.VMEM((3 * 64, STACK), BF),
            pltpu.VMEM((3 * STACK, 128), BF),
            pltpu.VMEM((PIECE, PIECE), BF),
            pltpu.VMEM((NV * PART, STACK), BF),
            pltpu.VMEM((NV, ROWS, CB), BF),
            pltpu.VMEM((NV, ROWS, CB), BF),
            pltpu.VMEM((32, 128), BF),
            pltpu.VMEM((NV, 32, 128), BF),
            pltpu.VMEM((NG, NV * PART, CB), BF),
            pltpu.VMEM((NV, NG, PART, CB), BF),
            pltpu.VMEM((NL, NG, PART, CB), BF),
            pltpu.VMEM((PAGES, 8, 128), F32),
            pltpu.VMEM((8, 8, 128), F32),
            pltpu.VMEM((2, PAGES, 8, 128), F32),
            pltpu.VMEM((2, 8, 128), F32),
            pltpu.VMEM((2, texels, 8, 128), F32),
            pltpu.VMEM((2, 8, 128), F32),
            pltpu.VMEM((2, 4, 8, 128), F32),
            dma((NG + 1,)), dma((NV,)), dma((NV,)), dma((NG, NV)), dma((NG, NV)), dma((NV,)), dma((NV,)),
            dma((NG, NV)), dma((NG, NL)), dma((PAGES,)), dma((2, PAGES)), dma((2, texels)), dma((2, texels)),
            dma((4,)), dma((2, 4)), dma((NL,)), dma((texels,)),
        ],
        compiler_params=pltpu.CompilerParams(
            collective_id=0, has_side_effects=True, vmem_limit_bytes=40 * 1024 * 1024
        ),
    )(pltpu.with_memory_space_constraint(slab, pltpu.HBM), pltpu.with_memory_space_constraint(basis, pltpu.HBM))
    return grams[0] * view_scale, core.reshape(RB, LB, 4 * CB), grams[1] * light_scale


def solution(mesh):
    return jax.shard_map(
        body,
        mesh=mesh,
        in_specs=(P("light", "view", "texel"), P("view", None)),
        out_specs=(P("view", None), P("view", "light", "texel"), P("light", None)),
        check_vma=False,
    )
```

```python
import jax
import jax.numpy as jnp
from jax import lax
from jax.experimental import pallas as pl
from jax.experimental.pallas import tpu as pltpu
from jax.sharding import PartitionSpec as P

MESH = pl.DeviceIdType.MESH
BF = jnp.bfloat16
F32 = jnp.float32
LB = 20
VB = 20
NV = 4
NL = 4
RB = 12
CB = 256
ROWS = LB * VB
PIECE = RB * LB
NG = 5
GROUP = 4 * VB
STACK = NV * GROUP
AHEAD = 4
PART = 4 * RB
PAGES = NL * NV


def cells(shape):
    return lax.broadcasted_iota(jnp.int32, shape, 0), lax.broadcasted_iota(jnp.int32, shape, 1)


def div20(x):
    return (x * 3277) >> 16


def ones_where(condition, dtype=BF):
    return jnp.where(condition, 1.0, 0.0).astype(dtype)


def expand_table():
    row, col = cells((NV * 32, STACK))
    line = div20(col)
    return ones_where(row == 32 * (line >> 2) + col - VB * line)


def spread_table():
    row, col = cells((NV * PART, 128))
    return ones_where((row >> 2) == col)


def light_mask():
    row, col = cells((NV * PART, STACK))
    return ones_where((row & 3) == (div20(col) & 3))


def order_table():
    row, col = cells((PIECE, PIECE))
    group = (col * 1366) >> 16
    rest = col - PART * group
    return ones_where(row == LB * (rest >> 2) + 4 * group + (rest & 3))


def gram_place(g, x):
    if g:
        return 4 * (x >> 4) + (x & 3), (x >> 2) & 3
    line = div20(x)
    return 20 * (line >> 2) + x - 20 * line, line & 3


def keep_table(g):
    row, col = cells((STACK, STACK))
    return ones_where(gram_place(g, row)[1] == gram_place(g, col)[1], F32)


def pick_table(g):
    row, col = cells((8 * PAGES, STACK))
    p, q = row >> 3, row & 7
    return ones_where((q < 5) & (5 * p + q == gram_place(g, col)[0]))


def gather_table(g):
    row, col = cells((STACK, 128))
    return ones_where(gram_place(g, row)[0] == col)


def packed_tables():
    row, col = cells((3 * 64, STACK))
    piece, p, q = row >> 6, (row >> 3) & 7, row & 7
    wanted = 10 * p + jnp.where(piece == 0, q, 8 + (q >> 1))
    here = (piece == 0) | ((q < 4) & ((q & 1) == piece - 1))
    pick = ones_where(here & (wanted == gram_place(1, col)[0]))
    row, col = cells((3 * STACK, 128))
    piece = jnp.where(row >= STACK, 1, 0) + jnp.where(row >= 2 * STACK, 1, 0)
    column = gram_place(1, row - STACK * piece)[0]
    place = jnp.where(piece == 0, column, column + 120 - 40 * piece)
    low = 40 * jnp.maximum(piece - 1, 0)
    fits = (piece == 0) | ((column >= low) & (column < low + 40))
    return pick, ones_where(fits & (place == col))


def odd_share(k, t):
    return lax.rem(lax.div(k + 1 - t, 2), 2)


def share_of(k, j):
    e, t = lax.div(j, 2), lax.rem(j, 2)
    return 2 * t + lax.rem(odd_share(k, t) + 1 - e, 2)


def member_for(k, b):
    t, u = lax.div(b, 2), lax.rem(b, 2)
    return 2 * lax.rem(odd_share(k, t) + 1 + u, 2) + t


def center_of(b, n):
    t, u = lax.div(b, 2), lax.rem(b, 2)
    z = lax.rem(1 + 4 * u + 2 * t + lax.div(n, 2), 8)
    return lax.div(z, 2), 2 * lax.rem(z, 2) + lax.rem(n, 2)


def split_dot(a, b):
    def parts(x):
        hi = x.astype(BF)
        return hi, (x - hi.astype(F32)).astype(BF)

    if a.dtype == BF:
        return sum(jnp.dot(a, p, preferred_element_type=F32) for p in parts(b))
    return sum(jnp.dot(p, b, preferred_element_type=F32) for p in parts(a))


def remote(src, dst, send, recv, device):
    return pltpu.make_async_remote_copy(
        src_ref=src, dst_ref=dst, send_sem=send, recv_sem=recv, device_id=device, device_id_type=MESH
    )


def kernel(
    slab_hbm, basis_hbm,
    gram_ref, core_ref,
    slab_ref, basis_ref, keep_ref, pick_ref, gather_ref, packed_pick_ref, packed_gather_ref, order_ref, weights,
    dense, share, own_basis, all_basis, pieces, core_land, light_land,
    pages, light_pages, z_land, part, t_land, whole, last_land,
    load, basis_send, basis_recv, slab_send, slab_recv, core_send, core_recv,
    light_send, light_recv, z_send, z_recv, t_send, t_recv, last_send, last_recv, vz_send, vlast_send,
):
    texels = lax.axis_size("texel")
    tex, i, j = lax.axis_index("texel"), lax.axis_index("light"), lax.axis_index("view")
    me = i * NV + j
    mine = share_of(i, j)

    load_basis = pltpu.make_async_copy(basis_hbm, basis_ref, load.at[NG])
    load_basis.start()
    load_slab = [
        pltpu.make_async_copy(slab_hbm.at[4 * g : 4 * g + 4], slab_ref.at[4 * g : 4 * g + 4], load.at[g])
        for g in range(NG)
    ]
    for copy in load_slab:
        copy.start()
    barrier = pltpu.get_barrier_semaphore()

    def greet(device):
        pl.semaphore_signal(barrier, inc=1, device_id=device, device_id_type=MESH)

    for o in (1, 2, 3):
        greet((tex, i, lax.rem(j + o, NV)))
    for d in (2, 1, 3):
        for o in range(NV):
            greet((tex, lax.rem(i + d, NL), o))
    for o in range(1, texels):
        greet((lax.rem(tex + o, texels), i, j))

    own_basis[...] = jnp.zeros_like(own_basis)
    load_basis.wait()
    own_basis[0:VB, 0 : NV * RB] = basis_ref[...]

    def lay_out(g):
        load_slab[g].wait()
        for n in range(NV):
            for l in range(4 * g, 4 * g + 4):
                dense[n, l * VB : (l + 1) * VB, :] = slab_ref[l, :, n * CB : (n + 1) * CB]

    lay_out(0)
    pl.semaphore_wait(barrier, PAGES - 1 + texels - 1)

    others = [j, j + 1 - 2 * lax.rem(j, 2), lax.rem(j + 2, NV), NV - 1 - j]
    shares = [share_of(i, other) for other in others]

    def rows_of(g):
        return pl.ds(g * GROUP, GROUP)

    def part_of(p):
        return pl.ds(pl.multiple_of(p * PART, 16), PART)

    def slab_copy(g, o, slot):
        return remote(
            dense.at[shares[o], rows_of(g), :], share.at[slot, rows_of(g), :], slab_send.at[g, o],
            slab_recv.at[g, slot], (tex, i, others[o]),
        )

    def basis_copy(o, slot):
        return remote(own_basis, all_basis.at[slot], basis_send.at[o], basis_recv.at[slot], (tex, i, others[o]))

    for o in (2, 3, 1):
        basis_copy(o, j).start()
    local = [
        pltpu.make_async_copy(dense.at[mine, rows_of(g), :], share.at[j, rows_of(g), :], slab_recv.at[g, j])
        for g in range(NG)
    ]

    def slab_start(g):
        for o in (2, 3, 1):
            slab_copy(g, o, j).start()
        local[g].start()

    for g in range(NG):
        if g:
            lay_out(g)
        if g < AHEAD:
            slab_start(g)
    all_basis[j] = own_basis[...]
    spread, expand, mask = spread_table(), expand_table(), light_mask()
    for o in (1, 2, 3):
        basis_copy(o, others[o]).wait_recv()

    table = lax.dot_general(
        all_basis[...].reshape(NV * 32, 128), expand, (((0,), (0,)), ((), ())), preferred_element_type=F32
    ).astype(BF)
    weights[...] = jnp.dot(spread, table, preferred_element_type=F32).astype(BF) * mask

    ahead = lax.rem(1 + 4 * lax.rem(mine, 2) + 2 * lax.div(mine, 2) - 2 * i - lax.div(j, 2) + 8, 8)
    far = 1 - lax.div(ahead, 4)
    turns = [2 * far, 2 * far + 1, 2 * (1 - far), 2 * (1 - far) + 1]
    centers = [center_of(mine, p) for p in turns]

    def light_copy(g, o, ci, cj):
        return remote(
            pieces.at[g, part_of(turns[o]), :], light_land.at[i, g], light_send.at[g, o], light_recv.at[g, i],
            (tex, ci, cj),
        )

    def core_copy(o, slot, place):
        return remote(
            pieces.at[:, part_of(others[o]), :], core_land.at[place], core_send.at[o], core_recv.at[slot],
            (tex, i, others[o]),
        )

    def stack_of(g):
        return jnp.concatenate([share[s, g * GROUP : (g + 1) * GROUP, :] for s in range(NV)], axis=0)

    for g in range(NG):
        local[g].wait()
        for o in (1, 2, 3):
            slab_copy(g, o, others[o]).wait_recv()
        if g + AHEAD < NG:
            slab_start(g + AHEAD)
        pieces[g] = jnp.dot(weights[...], stack_of(g), preferred_element_type=F32).astype(BF)
        for o in range(NV):
            ci, cj = centers[o]
            here = jnp.logical_and(ci == i, cj == j)

            @pl.when(here)
            def _():
                pltpu.make_async_copy(
                    pieces.at[g, part_of(turns[o]), :], light_land.at[i, g], light_recv.at[g, i]
                ).start()

            @pl.when(jnp.logical_not(here))
            def _():
                light_copy(g, o, ci, cj).start()

    def products(stacks):
        wide = jnp.concatenate(list(stacks), axis=1)
        return lax.dot_general(wide, wide, (((1,), (1,)), ((), ())), preferred_element_type=F32)

    def to_pages(total):
        rows = split_dot(pick_ref[...], total * keep_ref[0])
        return split_dot(rows, gather_ref[...]).reshape(PAGES, 8, 128)

    def to_packed(total):
        rows = split_dot(packed_pick_ref[...], total * keep_ref[1])
        return sum(
            split_dot(rows[64 * n : 64 * n + 64], packed_gather_ref[STACK * n : STACK * n + STACK, :])
            for n in range(3)
        ).reshape(8, 8, 128)

    x, y = lax.div(tex, 4), lax.rem(tex, 4)

    def texel_at(o):
        return 4 * lax.rem(x + o // 4, 4) + lax.rem(y + o % 4, 4)

    sums = jnp.logical_or(j == 0, j == 3)
    core = lax.div(j, 2)

    def z_copy(d, c):
        ci = lax.rem(i + d, NL)
        return remote(
            light_pages.at[2 * ci + c], z_land.at[1, me], z_send.at[2 * d + c], z_recv.at[1, me], (tex, ci, 3 * c)
        )

    def z_landed(o):
        source = lax.rem(me + o, PAGES)
        return remote(
            light_pages.at[0], z_land.at[1, source], z_send.at[0], z_recv.at[1, source], (tex, i, others[1])
        )

    def t_copy(o, slot):
        other = texel_at(o)
        return remote(
            part.at[1], t_land.at[1, slot(other)], t_send.at[1, o], t_recv.at[1, slot(other)], (other, i, j)
        )

    def last_copy(o):
        return remote(
            whole.at[1], last_land.at[1, core], last_send.at[o], last_recv.at[1, core], (tex, i, others[o])
        )

    def last_landed(c):
        return remote(
            whole.at[1], last_land.at[1, c], last_send.at[1], last_recv.at[1, c], (tex, i, others[1])
        )

    takes = j == x

    def vt_copy(o, slot):
        other = texel_at(o)
        return remote(
            pages.at[other], t_land.at[0, slot(other)], t_send.at[0, o], t_recv.at[0, slot(other)], (other, i, j)
        )

    def vz_copy(o, slot):
        return remote(
            part.at[0], z_land.at[0, slot], vz_send.at[o], z_recv.at[0, slot], (tex, lax.rem(i + o, NL), x)
        )

    def vlast_copy(o, slot):
        return remote(
            whole.at[0], last_land.at[0, slot], vlast_send.at[o], last_recv.at[0, slot], (texel_at(o), i, j)
        )

    def start_all(copy, order, own):
        for o in order:
            copy(o, lambda other: own).start()

    def wait_all(copy, order):
        for o in order:
            copy(o, lambda other: other).wait_recv()

    def sent_all(copy, order, own):
        for o in order:
            copy(o, lambda other: own).wait_send()

    z_order = (8, 7, 9, 6, 10, 5, 11, 4, 12, 3, 13, 2, 14, 1, 15)
    t_order = (10, 9, 11, 6, 14, 8, 2, 5, 7, 13, 15, 4, 12, 1, 3)

    for g in range(2):
        keep_ref[g] = keep_table(g)
    pick_ref[...] = pick_table(0)
    gather_ref[...] = gather_table(0)
    packed_pick_ref[...], packed_gather_ref[...] = packed_tables()
    pages[...] = to_pages(products(stack_of(g) for g in range(NG)))
    start_all(vt_copy, t_order, tex)
    t_land[0, tex] = pages[tex]

    for o in (2, 3, 1):
        core_copy(o, j, mine).start()
    own_piece = pltpu.make_async_copy(pieces.at[:, part_of(j), :], core_land.at[mine], core_recv.at[j])
    own_piece.start()
    order_ref[...] = order_table()

    for g in range(NG):
        for k in range(NL):
            pltpu.make_async_copy(pieces.at[g, part_of(0), :], light_land.at[k, g], light_recv.at[g, k]).wait()
    light_pages[...] = to_packed(products(
        jnp.concatenate(
            [light_land[k, g, 16 * m : 16 * m + 16, :] for k in range(NL) for g in range(NG)], axis=0
        )
        for m in range(PART // 16)
    ))
    for d in (2, 1, 3):
        for c in range(2):
            z_copy(d, c).start()
    for c in range(2):
        @pl.when(j == 3 * c)
        def _():
            z_land[1, me] = light_pages[2 * i + c]

        @pl.when(j != 3 * c)
        def _():
            z_copy(0, c).start()


    wait_all(vt_copy, t_order)
    part[0] = jnp.sum(t_land[0], axis=0)
    for o in (2, 1, 3):
        vz_copy(o, me).start()

    @pl.when(takes)
    def _():
        z_land[0, me] = part[0]

    @pl.when(jnp.logical_not(takes))
    def _():
        vz_copy(0, me).start()

    for o in (1, 2, 3):
        basis_copy(o, j).wait_send()
        for g in range(NG):
            slab_copy(g, o, j).wait_send()
    for o in range(NV):
        ci, cj = centers[o]

        @pl.when(jnp.logical_not(jnp.logical_and(ci == i, cj == j)))
        def _():
            for g in range(NG):
                light_copy(g, o, ci, cj).wait_send()

    sent_all(vt_copy, t_order, tex)
    @pl.when(sums)
    def _():
        for o in z_order:
            z_landed(o).wait_recv()
        part[1] = jnp.sum(z_land[1], axis=0)
        start_all(t_copy, t_order, tex)
        t_land[1, tex] = part[1]

    @pl.when(takes)
    def _():
        for o in z_order:
            vz_copy(0, lax.rem(me + o, PAGES)).wait_recv()
        whole[0] = jnp.sum(z_land[0], axis=0)
        for o in t_order:
            vlast_copy(o, y).start()
        last_land[0, y] = whole[0]

    own_piece.wait()
    for o in (1, 2, 3):
        core_copy(o, others[o], shares[o]).wait_recv()
    for n in range(NV):
        core_ref[:, n * CB : (n + 1) * CB] = jnp.dot(
            order_ref[...], core_land[n].reshape(PIECE, CB), preferred_element_type=F32
        ).astype(BF)
    for o in (1, 2, 3):
        core_copy(o, j, mine).wait_send()
        vz_copy(o, me).wait_send()

    @pl.when(jnp.logical_not(takes))
    def _():
        vz_copy(0, me).wait_send()

    for d in (2, 1, 3):
        for c in range(2):
            z_copy(d, c).wait_send()
    for c in range(2):
        @pl.when(j != 3 * c)
        def _():
            z_copy(0, c).wait_send()

    @pl.when(sums)
    def _():
        wait_all(t_copy, t_order)
        whole[1] = jnp.sum(t_land[1], axis=0)
        for o in (2, 3, 1):
            last_copy(o).start()
        last_land[1, core] = whole[1]

    for q in range(4):
        @pl.when(jnp.logical_not(jnp.logical_and(takes, y == q)))
        def _():
            vlast_copy(1, q).wait_recv()

    @pl.when(takes)
    def _():
        for o in t_order:
            vlast_copy(o, y).wait_send()

    @pl.when(sums)
    def _():
        sent_all(t_copy, t_order, tex)

    for q in range(4):
        gram_ref[0, 5 * q : 5 * q + 5, :] = last_land[0, q, 0:5, 0:80]
    for c in range(2):
        @pl.when(j != 3 * c)
        def _():
            last_landed(c).wait_recv()

    @pl.when(sums)
    def _():
        for o in (2, 3, 1):
            last_copy(o).wait_send()

    for c in range(2):
        gram_ref[1, 10 * c : 10 * c + 8, :] = last_land[1, c, :, 0:80]
        for q in range(4):
            at = 10 * c + 8 + q // 2
            gram_ref[1, at : at + 1, 40 * (q % 2) : 40 * (q % 2) + 40] = last_land[1, c, q : q + 1, 80:120]


def body(slab, basis):
    texels = lax.axis_size("texel")
    columns_all = slab.shape[2] * texels
    view_scale = 1.0 / (LB * NL * columns_all)
    light_scale = 1.0 / (RB * NV * columns_all)
    hbm = pl.BlockSpec(memory_space=pltpu.HBM)
    vmem = pl.BlockSpec(memory_space=pltpu.VMEM)
    dma = pltpu.SemaphoreType.DMA
    grams, core = pl.pallas_call(
        kernel,
        out_shape=(
            pltpu.VMEM((2, VB, 80), F32),
            pltpu.VMEM((PIECE, 4 * CB), BF),
        ),
        in_specs=[hbm] * 2,
        out_specs=(vmem,) * 2,
        scratch_shapes=[
            pltpu.VMEM(slab.shape, BF),
            pltpu.VMEM(basis.shape, BF),
            pltpu.VMEM((2, STACK, STACK), F32),
            pltpu.VMEM((8 * PAGES, STACK), BF),
            pltpu.VMEM((STACK, 128), BF),
            pltpu.VMEM((3 * 64, STACK), BF),
            pltpu.VMEM((3 * STACK, 128), BF),
            pltpu.VMEM((PIECE, PIECE), BF),
            pltpu.VMEM((NV * PART, STACK), BF),
            pltpu.VMEM((NV, ROWS, CB), BF),
            pltpu.VMEM((NV, ROWS, CB), BF),
            pltpu.VMEM((32, 128), BF),
            pltpu.VMEM((NV, 32, 128), BF),
            pltpu.VMEM((NG, NV * PART, CB), BF),
            pltpu.VMEM((NV, NG, PART, CB), BF),
            pltpu.VMEM((NL, NG, PART, CB), BF),
            pltpu.VMEM((PAGES, 8, 128), F32),
            pltpu.VMEM((8, 8, 128), F32),
            pltpu.VMEM((2, PAGES, 8, 128), F32),
            pltpu.VMEM((2, 8, 128), F32),
            pltpu.VMEM((2, texels, 8, 128), F32),
            pltpu.VMEM((2, 8, 128), F32),
            pltpu.VMEM((2, 4, 8, 128), F32),
            dma((NG + 1,)), dma((NV,)), dma((NV,)), dma((NG, NV)), dma((NG, NV)), dma((NV,)), dma((NV,)),
            dma((NG, NV)), dma((NG, NL)), dma((PAGES,)), dma((2, PAGES)), dma((2, texels)), dma((2, texels)),
            dma((4,)), dma((2, 4)), dma((NL,)), dma((texels,)),
        ],
        compiler_params=pltpu.CompilerParams(
            collective_id=0, has_side_effects=True, vmem_limit_bytes=40 * 1024 * 1024
        ),
    )(pltpu.with_memory_space_constraint(slab, pltpu.HBM), pltpu.with_memory_space_constraint(basis, pltpu.HBM))
    return grams[0] * view_scale, core.reshape(RB, LB, 4 * CB), grams[1] * light_scale


def solution(mesh):
    return jax.shard_map(
        body,
        mesh=mesh,
        in_specs=(P("light", "view", "texel"), P("view", None)),
        out_specs=(P("view", None), P("view", "light", "texel"), P("light", None)),
        check_vma=False,
    )
```
